32 devices in a mesh: freq: 8 (over y, x, core), beam: 4 (over z).
Axes of the slice: x: 2, y: 2, z: 4, core: 2. Of those that a mesh axis runs over, the one named last changes fastest.
Arguments:
- block_samples: bfloat16 [4, 2048, 256], P('beam', 'freq'), may hold values from -6 to 6
- tail_samples: bfloat16 [4, 2048, 2048], P('beam', 'freq'), may hold values from -6 to 6
- tail_blocks: int32 [4], P('beam'), may hold values from 1 to 16, as said below
- dm_limit: int32 [4], P('beam'), may hold values from 256 to 2048, as said below
Outputs:
- peak_snr: float32 [4, 7, 2048], P('beam', None, 'freq')
- excess_snr: float32 [4, 7, 2048], P('beam', None, 'freq')
The draws below stay inside these ranges and needn't reach their ends.
Inputs may be any that keep to these rules, and one draw needn't show every extreme that they name: `tail_blocks`: some beam has a full tail in every draw. `dm_limit`: some beam searches all trials in every draw.
All inputs are finite; a program needn't handle non-finite values.
Results may differ from the reference program's by a relative error of at most 0.0003.
Values sent between devices are 32-bit elements; how exact they have to be, the bound alone decides.
A program may use at most 64 MiB of HBM per device.

```python
import jax
import jax.numpy as jnp
from jax import lax

CHAN = 2048
BLOCK = 256
WIDTHS = 7
TAIL = 2048
BEAMS = 4


def draw_tail_blocks(key, part):
    most = TAIL // 128
    values = jax.random.randint(key, (BEAMS,), 1, most + 1, dtype=jnp.int32)
    chosen = jax.random.randint(jax.random.fold_in(key, 11), (), 0, BEAMS, dtype=jnp.int32)
    return values.at[chosen].set(most)


def draw_dm_limit(key, part):
    values = jax.random.randint(key, (BEAMS,), CHAN // 8, CHAN + 1, dtype=jnp.int32)
    chosen = jax.random.randint(jax.random.fold_in(key, 23), (), 0, BEAMS, dtype=jnp.int32)
    return values.at[chosen].set(CHAN)


def steps_of(rng, shape, cuts, low, high):
    def one(dim, parts):
        heights = jax.random.uniform(jax.random.fold_in(jax.random.fold_in(rng, 6), dim), (parts,), jnp.float32, low / len(cuts), high / len(cuts))
        return jnp.repeat(jnp.exp(heights), shape[dim] // parts).reshape((-1,) + (1,) * (len(shape) - dim - 1))

    level = one(*cuts[0])
    for cut in cuts[1:]:
        level = level * one(*cut)
    return level


def scatter_about(rng, dims, width, limit, cuts=(), held_as=jnp.bfloat16):
    result = width * jax.random.normal(rng, dims, jnp.float32)
    if cuts:
        result = result * steps_of(rng, dims, cuts, -0.22, 0.18)
    return jnp.clip(result, -limit, limit).astype(held_as)


def setup_inputs(seed: int = 0) -> dict:
    arg_keys = jax.random.split(jax.random.key(seed), 5)
    return {
        "block_samples": scatter_about(arg_keys[0], (BEAMS, CHAN, BLOCK), 1.0, 6.0, ((0, 4), (1, 8))),
        "tail_samples": scatter_about(arg_keys[1], (BEAMS, CHAN, TAIL), 1.0, 6.0, ((0, 4), (1, 8))),
        "tail_blocks": draw_tail_blocks(jax.random.fold_in(arg_keys[4], 71), 0),
        "dm_limit": draw_dm_limit(jax.random.fold_in(arg_keys[4], 71), 0),
    }


def delay_rows(series, shifts, reach_max):
    dims_of = series.shape
    flattened = series.reshape((-1,) + dims_of[-2:])
    padded = jnp.pad(flattened, ((0, 0), (0, 0), (reach_max, 0)))

    def slide_row(single_row, amount):
        return lax.dynamic_slice_in_dim(single_row, reach_max - amount, dims_of[-1], axis=1)
    moved_rows = jax.vmap(slide_row, in_axes=(1, 0), out_axes=1)(padded, shifts)
    return moved_rows.reshape(dims_of)

def tree_section(series, offset, reach_max):
    upper_half = jnp.repeat(series[..., 0::2, :, :], 2, axis=-2)
    lower_half = jnp.repeat(series[..., 1::2, :, :], 2, axis=-2)
    out_rows = upper_half.shape[-2]
    trials = offset + jnp.arange(out_rows, dtype=jnp.int32)
    shifts = (trials - trials // 2).astype(jnp.int32)
    return upper_half + delay_rows(lower_half, shifts, reach_max)

def peak_ratios(series, tail_len):
    searched = series[..., tail_len:]
    average = lax.optimization_barrier(jnp.mean(searched, axis=-1, keepdims=True))
    deviation = jnp.sqrt(lax.optimization_barrier(jnp.mean((searched - average) ** 2, axis=-1, keepdims=True)) + 1e-05)
    boxcar = series
    results = []
    for width_bit in range(WIDTHS):
        width_now = 2 ** width_bit
        if width_bit > 0:
            half_width = width_now // 2
            pad_spec = [(0, 0)] * (series.ndim - 1) + [(half_width, 0)]
            boxcar = boxcar + jnp.pad(boxcar[..., :-half_width], pad_spec)
        ratio = (boxcar[..., tail_len:] - width_now * average) / (jnp.sqrt(jnp.float32(width_now)) * deviation)
        results.append(lax.optimization_barrier(jnp.max(ratio, axis=-1)))
    return jnp.stack(results, axis=-2)

def reference(block_samples, tail_samples, tail_blocks, dm_limit):
    tail_len = tail_samples.shape[-1]

    def per_beam(pieces):
        block_row, tail_row, tail_count, limit_val = pieces
        valid_mask = jnp.arange(tail_len, dtype=jnp.int32)[None, :] >= tail_len - 128 * tail_count
        joined = jnp.concatenate([jnp.where(valid_mask, tail_row.astype(jnp.float32), jnp.float32(0.0)), block_row.astype(jnp.float32)], axis=-1)
        series = joined[:, None, :]
        while series.shape[0] > 1:
            series = tree_section(series, 0, series.shape[1])
        scores = peak_ratios(series[0], tail_len)
        trial_ids = jnp.arange(scores.shape[-1], dtype=jnp.int32)
        return jnp.where(trial_ids[None, :] < limit_val, scores, jnp.float32(0.0))
    peak_snr = lax.map(per_beam, (block_samples, tail_samples, tail_blocks, dm_limit))
    excess_snr = peak_snr - lax.optimization_barrier(jnp.sum(peak_snr, axis=0, keepdims=True)) / peak_snr.shape[0]
    return (peak_snr, excess_snr)
```

```python
import functools

import jax
import jax.numpy as jnp
import numpy as np
from jax import lax
from jax.experimental import pallas as pl
from jax.experimental.pallas import tpu as pltpu
from jax.sharding import PartitionSpec as P

WIDTHS = 7


def partner_2(block, axis, stride):
    count = lax.axis_size(axis)
    route = []
    for low in range(count):
        high = low | 1 << stride
        if high != low and high < count:
            route += [(low, high), (high, low)]
    return lax.ppermute(block, axis, route)


def skew_rows(series, step_size, base_shift, pad_width):
    dims_of = series.shape
    rows_count = dims_of[-2]
    length_now = dims_of[-1]
    flattened = series.reshape((-1, rows_count, length_now))
    padded = jnp.pad(flattened, ((0, 0), (0, 0), (pad_width, 0)))
    row_width = length_now + pad_width
    lined_up = padded.reshape((flattened.shape[0], rows_count * row_width))
    lined_up = jnp.pad(lined_up, ((0, 0), (0, pad_width)))
    window = lax.dynamic_slice_in_dim(
        lined_up, pad_width - base_shift, rows_count * (row_width - step_size), axis=1
    )
    moved_rows = window.reshape((flattened.shape[0], rows_count, row_width - step_size))[
        :, :, :length_now
    ]
    return moved_rows.reshape(dims_of)


def tree_section(series, offset, reach_max):
    upper_rows = series[..., 0::2, :, :]
    odd_rows = series[..., 1::2, :, :]
    even_moved = skew_rows(odd_rows, 1, (offset + 1) // 2, reach_max)
    odd_moved = skew_rows(odd_rows, 1, (offset + 2) // 2, reach_max)
    joined_rows = jnp.stack([upper_rows + even_moved, upper_rows + odd_moved], axis=-2)
    dims_of = upper_rows.shape
    return joined_rows.reshape(dims_of[:-2] + (2 * dims_of[-2], dims_of[-1]))


def peak_ratios(series, tail_len):
    searched = series[..., tail_len:]
    average = jnp.mean(searched, axis=-1, keepdims=True)
    deviation = jnp.sqrt(jnp.mean((searched - average) ** 2, axis=-1, keepdims=True) + 1e-05)
    reach_back = 2 ** (WIDTHS - 1)
    boxcar = series[..., tail_len - reach_back :]
    results = []
    for width_bit in range(WIDTHS):
        width_now = 2**width_bit
        if width_bit > 0:
            half_width = width_now // 2
            pad_spec = [(0, 0)] * (series.ndim - 1) + [(half_width, 0)]
            boxcar = boxcar + jnp.pad(boxcar[..., :-half_width], pad_spec)
        ratio = (boxcar[..., reach_back:] - width_now * average) / (
            jnp.sqrt(jnp.float32(width_now)) * deviation
        )
        results.append(jnp.max(ratio, axis=-1))
    return jnp.stack(results, axis=-2)


def local(block_samples, tail_samples, tail_blocks, dm_limit):
    beams_dev, local_chan, block_len = block_samples.shape
    tail_len = tail_samples.shape[2]
    valid_mask = (
        jnp.arange(tail_len, dtype=jnp.int32)[None, None, :]
        >= tail_len - 128 * tail_blocks[:, None, None]
    )
    joined = jnp.concatenate(
        [
            jnp.where(valid_mask, tail_samples.astype(jnp.float32), jnp.float32(0.0)),
            block_samples.astype(jnp.float32),
        ],
        axis=-1,
    )
    series = joined[:, :, None, :]
    while series.shape[1] > 1:
        series = tree_section(series, 0, series.shape[2])
    devices = lax.axis_size("freq")
    position = lax.axis_index("freq")
    level_count = devices.bit_length() - 1
    dm_rows = series[:, 0]
    rank_now = jnp.zeros((), jnp.int32)
    for level_bit in range(level_count):
        group_size = 1 << level_bit
        partner = partner_2(dm_rows, "freq", level_bit)
        side_bit = position // group_size % 2
        rank_now = 2 * rank_now + side_bit
        mine_first = side_bit == 0
        upper_half = jnp.where(mine_first, dm_rows, partner)
        lower_half = jnp.where(mine_first, partner, dm_rows)
        base_shift = (rank_now + 1) // 2
        dm_rows = upper_half + skew_rows(
            lower_half, group_size, base_shift, group_size * local_chan
        )
    scores = peak_ratios(dm_rows, tail_len)
    received = lax.all_to_all(scores[..., None], "freq", split_axis=2, concat_axis=3, tiled=True)
    sources = np.arange(devices)
    reorder = np.zeros(devices, dtype=np.int32)
    for level_bit in range(level_count):
        reorder = reorder + ((sources >> level_bit & 1) << level_count - 1 - level_bit).astype(
            np.int32
        )
    received = jnp.take(received, jnp.asarray(reorder), axis=3)
    scores = received.reshape((beams_dev, WIDTHS, local_chan))
    trial_ids = position * local_chan + jnp.arange(local_chan, dtype=jnp.int32)
    peak_snr = jnp.where(
        trial_ids[None, None, :] < dm_limit[:, None, None], scores, jnp.float32(0.0)
    )
    beam_total = lax.psum(jnp.sum(peak_snr, axis=0), "beam")
    excess_snr = peak_snr - beam_total[None] / (beams_dev * lax.axis_size("beam"))
    return (peak_snr, excess_snr)


LANES = 128
MESH_ID = pl.DeviceIdType.MESH


def windows(total_levels, keep, span):
    return [
        min(-(-(keep + 2 ** (total_levels - s) - 1) // LANES), span + 1)
        for s in range(total_levels + 1)
    ]


def late_tiles(later, earlier, amount):
    lane = lax.broadcasted_iota(jnp.int32, (8, LANES), 1)
    return jnp.where(lane < amount, earlier, later)


def shift_uniform(tiles, amount):
    rolled = [pltpu.roll(x, amount, 1) for x in tiles]
    lane = lax.broadcasted_iota(jnp.int32, (8, LANES), 1)
    head = lane < amount
    return [
        jnp.where(head, rolled[max(i - 1, 0)], rolled[i]) for i in range(len(tiles))
    ]


def merge_uniform(first, second, amount):
    even = [a + b for a, b in zip(first, second)]
    if isinstance(amount, int) and amount == 0:
        late_first = first
    else:
        late_first = shift_uniform(first, amount)
    late_second = shift_uniform(second, amount + 1)
    odd = [a + b for a, b in zip(late_first, late_second)]
    return even, odd


def fused(
    levels,
    cross,
    devices,
    beams,
    win,
    tail_tiles,
    block_tiles,
    tb_ref,
    lim_ref,
    block_ref,
    tail_ref,
    peak_ref,
    excess_ref,
    split_ref,
    *rest,
):
    stage_refs = rest[: levels - 4]
    turn_ref, send_ref, recv_ref, snr_ref, beam_ref = rest[levels - 4 : levels + 1]
    send_sem, recv_sem, bsend_sem, brecv_sem = rest[levels + 1 :]
    me = lax.axis_index("freq")
    my_beam = lax.axis_index("beam")
    chan = 1 << levels
    half = chan // 2
    rows = chan // devices

    barrier = pltpu.get_barrier_semaphore()
    for o in range(1, devices):
        pl.semaphore_signal(
            barrier, inc=1, device_id={"freq": lax.rem(me + o, devices)}, device_id_type=MESH_ID
        )
    for o in range(1, beams):
        pl.semaphore_signal(
            barrier, inc=1, device_id={"beam": lax.rem(my_beam + o, beams)}, device_id_type=MESH_ID
        )

    groups = half // 8
    row = lax.broadcasted_iota(jnp.int32, (chan, chan), 0)
    col = lax.broadcasted_iota(jnp.int32, (chan, chan), 1)
    inner = row % half
    wanted = 2 * ((inner % 8) * groups + inner // 8) + row // half
    pick = jnp.where(col == wanted, 1.0, 0.0).astype(jnp.bfloat16)
    first_valid = tail_tiles - tb_ref[0]
    split_ref[0] = jnp.zeros((chan, LANES), jnp.float32)
    for w in range(0, tail_tiles, 2):
        part = jnp.dot(
            pick, tail_ref[0, :, LANES * w : LANES * (w + 2)], preferred_element_type=jnp.float32
        )
        for i in range(2):
            gain = jnp.where(w + i >= first_valid, 1.0, 0.0).astype(jnp.float32)
            split_ref[1 + w + i] = part[:, LANES * i : LANES * (i + 1)] * gain
    for w in range(0, block_tiles, 2):
        part = jnp.dot(
            pick, block_ref[0, :, LANES * w : LANES * (w + 2)], preferred_element_type=jnp.float32
        )
        for i in range(2):
            split_ref[1 + tail_tiles + w + i] = part[:, LANES * i : LANES * (i + 1)]

    lane_row = lax.broadcasted_iota(jnp.int32, (8, LANES), 0)

    def delayed(load_first, load_second, base, stride, out_tiles, in_tiles):
        whole = base // LANES
        short = base % LANES
        start = in_tiles - out_tiles - whole - 1
        first, second = load_first(start, out_tiles + 1), load_second(start, out_tiles + 1)
        dims = first.shape
        flat = (dims[0] * dims[1], 8, LANES)
        turned = pltpu.roll(second.reshape(flat), 1, 2).reshape(dims)
        earlier = jnp.concatenate([turned[:, :1], turned[:, :-1]], axis=1)
        both = first + late_tiles(turned, earlier, 1)
        rolled = pltpu.roll(both.reshape(flat), short, 2)
        rolled = pltpu.roll(rolled, 0, 2, stride=stride, stride_axis=1).reshape(dims)
        return late_tiles(rolled[:, 1:], rolled[:, :-1], short + stride * lane_row)

    for s in range(levels - 3):
        out_groups = 1 << (levels - 4 - s)
        in_tiles, out_tiles = win[s], win[s + 1]
        low = in_tiles - out_tiles
        unit = 1 << (levels - 1 - s)
        trials = 1 << s

        def level_group(g, _, s=s, in_tiles=in_tiles, out_tiles=out_tiles, low=low, unit=unit,
                        out_groups=out_groups, trials=trials):
            if s == 0:
                def load_first(start, count):
                    return split_ref[pl.ds(start, count), pl.ds(pl.multiple_of(8 * g, 8), 8), :][None]

                def load_second(start, count):
                    return split_ref[
                        pl.ds(start, count), pl.ds(pl.multiple_of(half + 8 * g, 8), 8), :
                    ][None]
            else:
                source = stage_refs[s - 1]

                def load_first(start, count):
                    return source[2 * g, :, pl.ds(start, count)]

                def load_second(start, count):
                    return source[2 * g + 1, :, pl.ds(start, count)]

            even = load_first(low, out_tiles) + load_second(low, out_tiles)
            base = me * unit + g
            odd = delayed(load_first, load_second, base, out_groups, out_tiles, in_tiles)
            if s + 1 < levels - 3:
                target = stage_refs[s]
                for e in range(trials):
                    target[g, 2 * e] = even[e]
                    target[g, 2 * e + 1] = odd[e]
            else:
                for e in range(trials):
                    for w in range(out_tiles):
                        turn_ref[w, 16 * e : 16 * e + 8] = even[e, w]
                        turn_ref[w, 16 * e + 8 : 16 * e + 16] = odd[e, w]
            return 0

        if out_groups == 1:
            level_group(0, 0)
        else:
            lax.fori_loop(0, out_groups, level_group, 0)

    pl.semaphore_wait(barrier, devices + beams - 2)
    tiles = win[levels]
    per = rows // 8
    dests = 8 // per

    def last_levels(q, _):
        nodes = [
            [
                [turn_ref[w, pl.ds(64 * q + n, 8, stride=8), :] for w in range(tiles)]
            ]
            for n in range(8)
        ]
        for s in range(3):
            merged = []
            for j in range(len(nodes) // 2):
                amount = me * (4 >> s) + j
                grown = []
                for a, b in zip(nodes[2 * j], nodes[2 * j + 1]):
                    even, odd = merge_uniform(a, b, amount)
                    grown += [even, odd]
                merged.append(grown)
            nodes = merged
        for c in range(8):
            for w in range(tiles):
                for h in range(dests):
                    send_ref[dests * q + h, w, pl.ds(c, per, stride=8), :] = nodes[0][c][w][
                        per * h : per * (h + 1)
                    ]
        return 0

    lax.fori_loop(0, chan // 64, last_levels, 0)

    copies = []
    for o in range(1, devices):
        target = lax.rem(me + o, devices)
        copy = pltpu.make_async_remote_copy(
            src_ref=send_ref.at[target],
            dst_ref=recv_ref.at[me],
            send_sem=send_sem.at[o],
            recv_sem=recv_sem.at[o],
            device_id={"freq": target},
            device_id_type=MESH_ID,
        )
        copy.start()
        copies.append(copy)
    recv_ref[me] = send_ref[me]
    for copy in copies:
        copy.wait()

    lane = lax.broadcasted_iota(jnp.int32, (8, LANES), 1)
    widths = jnp.ones((8, LANES), jnp.float32)
    roots = jnp.ones((8, LANES), jnp.float32)
    for i in range(WIDTHS):
        widths = jnp.where(lane == i, jnp.float32(2**i), widths)
        roots = jnp.where(lane == i, jnp.sqrt(jnp.float32(2**i)), roots)
    samples = block_tiles * LANES

    def finish(m, _):
        nodes = [
            [
                [recv_ref[j, w, pl.ds(pl.multiple_of(8 * m, 8), 8), :] for w in range(tiles)]
            ]
            for j in range(devices)
        ]
        for s in range(cross):
            merged = []
            for j in range(len(nodes) // 2):
                grown = []
                for a, b in zip(nodes[2 * j], nodes[2 * j + 1]):
                    even, odd = merge_uniform(a, b, j)
                    grown += [even, odd]
                merged.append(grown)
            nodes = merged
        for c in range(devices):
            series = nodes[0][c]
            block = series[tiles - block_tiles :]
            average = jnp.sum(sum(block), axis=1, keepdims=True) / samples
            variance = (
                jnp.sum(sum((x - average) ** 2 for x in block), axis=1, keepdims=True) / samples
            )
            deviation = jnp.sqrt(variance + 1e-05)
            peaks = jnp.zeros((8, LANES), jnp.float32)
            box = series
            for i in range(WIDTHS):
                if i > 0:
                    box = [x + y for x, y in zip(box, shift_uniform(box, 2 ** (i - 1)))]
                top = functools.reduce(jnp.maximum, box[tiles - block_tiles :])
                peaks = jnp.where(lane == i, jnp.max(top, axis=1, keepdims=True), peaks)
            ratio = (peaks - widths * average) / (roots * deviation)
            snr_ref[pl.ds(8 * devices * m + c, 8, stride=devices), :] = ratio
        return 0

    lax.fori_loop(0, rows // 8, finish, 0)

    peak = snr_ref[...].T[:8]
    trial = me * chan + lax.broadcasted_iota(jnp.int32, (8, chan), 1)
    peak = jnp.where(trial < lim_ref[0], peak, 0.0)
    beam_ref[my_beam] = peak
    copies = []
    for o in range(1, beams):
        copy = pltpu.make_async_remote_copy(
            src_ref=beam_ref.at[my_beam],
            dst_ref=beam_ref.at[my_beam],
            send_sem=bsend_sem.at[o],
            recv_sem=brecv_sem.at[o],
            device_id={"beam": lax.rem(my_beam + o, beams)},
            device_id_type=MESH_ID,
        )
        copy.start()
        copies.append(copy)
    peak_ref[0] = peak[:WIDTHS]
    for copy in copies:
        copy.wait()
    total = beam_ref[0]
    for b in range(1, beams):
        total = total + beam_ref[b]
    excess_ref[0] = (peak - total / beams)[:WIDTHS]


def fused_local(devices, beams, block_samples, tail_samples, tail_blocks, dm_limit):
    _, chan, block_len = block_samples.shape
    tail_len = tail_samples.shape[2]
    levels = chan.bit_length() - 1
    cross = devices.bit_length() - 1
    tail_tiles, block_tiles = tail_len // LANES, block_len // LANES
    win = windows(levels + cross, block_len + 2 ** (WIDTHS - 1) - 1, tail_tiles + block_tiles)
    rows = chan // devices
    scratch = [pltpu.VMEM((win[0], chan, LANES), jnp.float32)]
    for s in range(1, levels - 3):
        scratch.append(
            pltpu.VMEM((1 << (levels - 3 - s), 1 << s, win[s], 8, LANES), jnp.float32)
        )
    tiles = win[levels]
    scratch += [
        pltpu.VMEM((tiles, chan, LANES), jnp.float32),
        pltpu.VMEM((devices, tiles, rows, LANES), jnp.float32),
        pltpu.VMEM((devices, tiles, rows, LANES), jnp.float32),
        pltpu.VMEM((chan, LANES), jnp.float32),
        pltpu.VMEM((beams, 8, chan), jnp.float32),
        pltpu.SemaphoreType.DMA((devices,)),
        pltpu.SemaphoreType.DMA((devices,)),
        pltpu.SemaphoreType.DMA((beams,)),
        pltpu.SemaphoreType.DMA((beams,)),
    ]
    out = jax.ShapeDtypeStruct((1, WIDTHS, chan), jnp.float32)
    return pl.pallas_call(
        functools.partial(fused, levels, cross, devices, beams, win, tail_tiles, block_tiles),
        out_shape=(out, out),
        in_specs=[pl.BlockSpec(memory_space=pltpu.SMEM)] * 2
        + [pl.BlockSpec(memory_space=pltpu.VMEM)] * 2,
        out_specs=(pl.BlockSpec(memory_space=pltpu.VMEM),) * 2,
        scratch_shapes=scratch,
        compiler_params=pltpu.CompilerParams(
            collective_id=0, has_side_effects=True, vmem_limit_bytes=48 * 2**20
        ),
    )(tail_blocks, dm_limit, block_samples, tail_samples)


def fits(devices, beams_all, beams, chan):
    return beams_all == beams and chan % (8 * devices) == 0 and chan <= 64 * devices and chan >= 64


def solution(mesh):
    devices, beams = mesh.shape["freq"], mesh.shape["beam"]

    def body(block_samples, tail_samples, tail_blocks, dm_limit):
        args = (block_samples, tail_samples, tail_blocks, dm_limit)
        if fits(devices, beams * block_samples.shape[0], beams, block_samples.shape[1]):
            return fused_local(devices, beams, *args)
        return local(*args)

    return jax.shard_map(
        body,
        mesh=mesh,
        in_specs=(P("beam", "freq", None), P("beam", "freq", None), P("beam"), P("beam")),
        out_specs=(P("beam", None, "freq"), P("beam", None, "freq")),
        check_vma=False,
    )
```

```python
import functools

import jax
import jax.numpy as jnp
import numpy as np
from jax import lax
from jax.experimental import pallas as pl
from jax.experimental.pallas import tpu as pltpu
from jax.sharding import PartitionSpec as P

WIDTHS = 7


def partner_2(block, axis, stride):
    count = lax.axis_size(axis)
    route = []
    for low in range(count):
        high = low | 1 << stride
        if high != low and high < count:
            route += [(low, high), (high, low)]
    return lax.ppermute(block, axis, route)


def skew_rows(series, step_size, base_shift, pad_width):
    dims_of = series.shape
    rows_count = dims_of[-2]
    length_now = dims_of[-1]
    flattened = series.reshape((-1, rows_count, length_now))
    padded = jnp.pad(flattened, ((0, 0), (0, 0), (pad_width, 0)))
    row_width = length_now + pad_width
    lined_up = padded.reshape((flattened.shape[0], rows_count * row_width))
    lined_up = jnp.pad(lined_up, ((0, 0), (0, pad_width)))
    window = lax.dynamic_slice_in_dim(
        lined_up, pad_width - base_shift, rows_count * (row_width - step_size), axis=1
    )
    moved_rows = window.reshape((flattened.shape[0], rows_count, row_width - step_size))[
        :, :, :length_now
    ]
    return moved_rows.reshape(dims_of)


def tree_section(series, offset, reach_max):
    upper_rows = series[..., 0::2, :, :]
    odd_rows = series[..., 1::2, :, :]
    even_moved = skew_rows(odd_rows, 1, (offset + 1) // 2, reach_max)
    odd_moved = skew_rows(odd_rows, 1, (offset + 2) // 2, reach_max)
    joined_rows = jnp.stack([upper_rows + even_moved, upper_rows + odd_moved], axis=-2)
    dims_of = upper_rows.shape
    return joined_rows.reshape(dims_of[:-2] + (2 * dims_of[-2], dims_of[-1]))


def peak_ratios(series, tail_len):
    searched = series[..., tail_len:]
    average = jnp.mean(searched, axis=-1, keepdims=True)
    deviation = jnp.sqrt(jnp.mean((searched - average) ** 2, axis=-1, keepdims=True) + 1e-05)
    reach_back = 2 ** (WIDTHS - 1)
    boxcar = series[..., tail_len - reach_back :]
    results = []
    for width_bit in range(WIDTHS):
        width_now = 2**width_bit
        if width_bit > 0:
            half_width = width_now // 2
            pad_spec = [(0, 0)] * (series.ndim - 1) + [(half_width, 0)]
            boxcar = boxcar + jnp.pad(boxcar[..., :-half_width], pad_spec)
        ratio = (boxcar[..., reach_back:] - width_now * average) / (
            jnp.sqrt(jnp.float32(width_now)) * deviation
        )
        results.append(jnp.max(ratio, axis=-1))
    return jnp.stack(results, axis=-2)


def local(block_samples, tail_samples, tail_blocks, dm_limit):
    beams_dev, local_chan, block_len = block_samples.shape
    tail_len = tail_samples.shape[2]
    valid_mask = (
        jnp.arange(tail_len, dtype=jnp.int32)[None, None, :]
        >= tail_len - 128 * tail_blocks[:, None, None]
    )
    joined = jnp.concatenate(
        [
            jnp.where(valid_mask, tail_samples.astype(jnp.float32), jnp.float32(0.0)),
            block_samples.astype(jnp.float32),
        ],
        axis=-1,
    )
    series = joined[:, :, None, :]
    while series.shape[1] > 1:
        series = tree_section(series, 0, series.shape[2])
    devices = lax.axis_size("freq")
    position = lax.axis_index("freq")
    level_count = devices.bit_length() - 1
    dm_rows = series[:, 0]
    rank_now = jnp.zeros((), jnp.int32)
    for level_bit in range(level_count):
        group_size = 1 << level_bit
        partner = partner_2(dm_rows, "freq", level_bit)
        side_bit = position // group_size % 2
        rank_now = 2 * rank_now + side_bit
        mine_first = side_bit == 0
        upper_half = jnp.where(mine_first, dm_rows, partner)
        lower_half = jnp.where(mine_first, partner, dm_rows)
        base_shift = (rank_now + 1) // 2
        dm_rows = upper_half + skew_rows(
            lower_half, group_size, base_shift, group_size * local_chan
        )
    scores = peak_ratios(dm_rows, tail_len)
    received = lax.all_to_all(scores[..., None], "freq", split_axis=2, concat_axis=3, tiled=True)
    sources = np.arange(devices)
    reorder = np.zeros(devices, dtype=np.int32)
    for level_bit in range(level_count):
        reorder = reorder + ((sources >> level_bit & 1) << level_count - 1 - level_bit).astype(
            np.int32
        )
    received = jnp.take(received, jnp.asarray(reorder), axis=3)
    scores = received.reshape((beams_dev, WIDTHS, local_chan))
    trial_ids = position * local_chan + jnp.arange(local_chan, dtype=jnp.int32)
    peak_snr = jnp.where(
        trial_ids[None, None, :] < dm_limit[:, None, None], scores, jnp.float32(0.0)
    )
    beam_total = lax.psum(jnp.sum(peak_snr, axis=0), "beam")
    excess_snr = peak_snr - beam_total[None] / (beams_dev * lax.axis_size("beam"))
    return (peak_snr, excess_snr)


LANES = 128
PIECE = 512
UNROLL = 4
MESH_ID = pl.DeviceIdType.MESH


def windows(total_levels, keep, span):
    return [
        min(-(-(keep + 2 ** (total_levels - s) - 1) // LANES), span + 1)
        for s in range(total_levels + 1)
    ]


def late_tiles(later, earlier, amount):
    lane = lax.broadcasted_iota(jnp.int32, (8, LANES), 1)
    return jnp.where(lane < amount, earlier, later)


def shift_uniform(tiles, amount):
    rolled = [pltpu.roll(x, amount, 1) for x in tiles]
    lane = lax.broadcasted_iota(jnp.int32, (8, LANES), 1)
    head = lane < amount
    return [
        jnp.where(head, rolled[max(i - 1, 0)], rolled[i]) for i in range(len(tiles))
    ]


def merge_uniform(first, second, amount):
    even = [a + b for a, b in zip(first, second)]
    if isinstance(amount, int) and amount == 0:
        late_first = first
    else:
        late_first = shift_uniform(first, amount)
    late_second = shift_uniform(second, amount + 1)
    odd = [a + b for a, b in zip(late_first, late_second)]
    return even, odd


def fused(
    levels,
    cross,
    devices,
    beams,
    win,
    tail_tiles,
    block_tiles,
    tb_ref,
    lim_ref,
    block_ref,
    tail_ref,
    peak_ref,
    excess_ref,
    split_ref,
    *rest,
):
    stage_refs = rest[: levels - 4]
    turn_ref, send_ref, recv_ref, snr_ref, beam_ref, held_ref = rest[levels - 4 : levels + 2]
    load_sem, send_sem, recv_sem, bsend_sem, brecv_sem = rest[levels + 2 :]
    me = lax.axis_index("freq")
    my_beam = lax.axis_index("beam")
    chan = 1 << levels
    half = chan // 2
    rows = chan // devices
    tail_len, block_len = tail_tiles * LANES, block_tiles * LANES
    pieces = [(tail_ref, at, at, PIECE) for at in range(0, tail_len, PIECE)]
    pieces.append((block_ref, 0, tail_len, block_len))
    loads = []
    for i, (source, at, to, size) in enumerate(pieces):
        load = pltpu.make_async_copy(
            source.at[0, :, at : at + size], held_ref.at[:, to : to + size], load_sem.at[i]
        )
        load.start()
        loads.append(load)

    barrier = pltpu.get_barrier_semaphore()
    for o in range(1, devices):
        pl.semaphore_signal(
            barrier, inc=1, device_id={"freq": lax.rem(me + o, devices)}, device_id_type=MESH_ID
        )
    for o in range(1, beams):
        pl.semaphore_signal(
            barrier, inc=1, device_id={"beam": lax.rem(my_beam + o, beams)}, device_id_type=MESH_ID
        )

    groups = half // 8
    row = lax.broadcasted_iota(jnp.int32, (chan, chan), 0)
    col = lax.broadcasted_iota(jnp.int32, (chan, chan), 1)
    inner = row % half
    wanted = 2 * ((inner % 8) * groups + inner // 8) + row // half
    pick = jnp.where(col == wanted, 1.0, 0.0).astype(jnp.bfloat16)
    first_valid = tail_tiles - tb_ref[0]
    split_ref[0] = jnp.zeros((chan, LANES), jnp.float32)
    for i, (_, _, to, size) in enumerate(pieces):
        loads[i].wait()
        for w in range(to // LANES, (to + size) // LANES, 2):
            part = jnp.dot(
                pick, held_ref[:, LANES * w : LANES * (w + 2)], preferred_element_type=jnp.float32
            )
            for k in range(2):
                tile = part[:, LANES * k : LANES * (k + 1)]
                if w < tail_tiles:
                    tile = tile * jnp.where(w + k >= first_valid, 1.0, 0.0).astype(jnp.float32)
                split_ref[1 + w + k] = tile

    lane_row = lax.broadcasted_iota(jnp.int32, (8, LANES), 0)

    def delayed(load_first, load_second, base, stride, out_tiles, in_tiles):
        whole = base // LANES
        short = base % LANES
        start = in_tiles - out_tiles - whole - 1
        first, second = load_first(start, out_tiles + 1), load_second(start, out_tiles + 1)
        turned = pltpu.roll(second, 1, 2)
        earlier = jnp.concatenate([turned[:1], turned[:-1]], axis=0)
        both = first + late_tiles(turned, earlier, 1)
        rolled = pltpu.roll(both, short, 2)
        rolled = pltpu.roll(rolled, 0, 2, stride=stride, stride_axis=1)
        return late_tiles(rolled[1:], rolled[:-1], short + stride * lane_row)

    for s in range(levels - 3):
        out_groups = 1 << (levels - 4 - s)
        in_tiles, out_tiles = win[s], win[s + 1]
        low = in_tiles - out_tiles
        unit = 1 << (levels - 1 - s)
        trials = 1 << s

        def level_group(g, e, s=s, in_tiles=in_tiles, out_tiles=out_tiles, low=low, unit=unit,
                        out_groups=out_groups):
            if s == 0:
                def load_first(start, count):
                    return split_ref[pl.ds(start, count), pl.ds(pl.multiple_of(8 * g, 8), 8), :]

                def load_second(start, count):
                    return split_ref[
                        pl.ds(start, count), pl.ds(pl.multiple_of(half + 8 * g, 8), 8), :
                    ]
            else:
                source = stage_refs[s - 1]

                def load_first(start, count):
                    return source[2 * g, e, pl.ds(start, count)]

                def load_second(start, count):
                    return source[2 * g + 1, e, pl.ds(start, count)]

            even = load_first(low, out_tiles) + load_second(low, out_tiles)
            odd = delayed(load_first, load_second, me * unit + g, out_groups, out_tiles, in_tiles)
            if s + 1 < levels - 3:
                target = stage_refs[s]
                target[g, 2 * e] = even
                target[g, 2 * e + 1] = odd
            else:
                for w in range(out_tiles):
                    turn_ref[w, 16 * e : 16 * e + 8] = even[w]
                    turn_ref[w, 16 * e + 8 : 16 * e + 16] = odd[w]

        at_once = min(out_groups, UNROLL)

        def level_groups(i, _, level_group=level_group, at_once=at_once, trials=trials):
            for k in range(at_once):
                for e in range(trials):
                    level_group(at_once * i + k, e)
            return 0

        if out_groups == at_once:
            level_groups(0, 0)
        else:
            lax.fori_loop(0, out_groups // at_once, level_groups, 0)

    pl.semaphore_wait(barrier, devices + beams - 2)
    tiles = win[levels]
    per = rows // 8
    dests = 8 // per

    def last_levels(q):
        nodes = [
            [
                [turn_ref[w, pl.ds(pl.multiple_of(64 * q, 64) + n, 8, stride=8), :]
                    for w in range(tiles)
                ]
            ]
            for n in range(8)
        ]
        for s in range(3):
            merged = []
            for j in range(len(nodes) // 2):
                amount = me * (4 >> s) + j
                grown = []
                for a, b in zip(nodes[2 * j], nodes[2 * j + 1]):
                    even, odd = merge_uniform(a, b, amount)
                    grown += [even, odd]
                merged.append(grown)
            nodes = merged
        for c in range(8):
            for w in range(tiles):
                for h in range(dests):
                    send_ref[dests * q + h, w, pl.ds(c, per, stride=8), :] = nodes[0][c][w][
                        per * h : per * (h + 1)
                    ]

    def exchange(target, source):
        return pltpu.make_async_remote_copy(
            src_ref=send_ref.at[target],
            dst_ref=recv_ref.at[source],
            send_sem=send_sem.at[target],
            recv_sem=recv_sem.at[source],
            device_id={"freq": target},
            device_id_type=MESH_ID,
        )

    chunks = chan // 64
    own = me // dests
    for i in range(1, chunks):
        q = lax.rem(own + i, chunks)
        last_levels(q)
        for h in range(dests):
            exchange(dests * q + h, me).start()
    last_levels(own)
    for h in range(1, dests):
        exchange(dests * own + lax.rem(me + h, dests), me).start()
    recv_ref[me] = send_ref[me]
    for o in range(1, devices):
        other = lax.rem(me + o, devices)
        exchange(other, me).wait_send()
        exchange(other, other).wait_recv()

    lane = lax.broadcasted_iota(jnp.int32, (8, LANES), 1)
    widths = jnp.ones((8, LANES), jnp.float32)
    roots = jnp.ones((8, LANES), jnp.float32)
    for i in range(WIDTHS):
        widths = jnp.where(lane == i, jnp.float32(2**i), widths)
        roots = jnp.where(lane == i, jnp.sqrt(jnp.float32(2**i)), roots)
    samples = block_tiles * LANES

    def finish(m):
        nodes = [
            [
                [recv_ref[j, w, pl.ds(pl.multiple_of(8 * m, 8), 8), :] for w in range(tiles)]
            ]
            for j in range(devices)
        ]
        for s in range(cross):
            merged = []
            for j in range(len(nodes) // 2):
                grown = []
                for a, b in zip(nodes[2 * j], nodes[2 * j + 1]):
                    even, odd = merge_uniform(a, b, j)
                    grown += [even, odd]
                merged.append(grown)
            nodes = merged
        for c in range(devices):
            series = nodes[0][c]
            block = series[tiles - block_tiles :]
            average = jnp.sum(sum(block), axis=1, keepdims=True) / samples
            variance = (
                jnp.sum(sum((x - average) ** 2 for x in block), axis=1, keepdims=True) / samples
            )
            deviation = jnp.sqrt(variance + 1e-05)
            peaks = jnp.zeros((8, LANES), jnp.float32)
            box = series
            for i in range(WIDTHS):
                if i > 0:
                    box = [x + y for x, y in zip(box, shift_uniform(box, 2 ** (i - 1)))]
                top = functools.reduce(jnp.maximum, box[tiles - block_tiles :])
                peaks = jnp.where(lane == i, jnp.max(top, axis=1, keepdims=True), peaks)
            ratio = (peaks - widths * average) / (roots * deviation)
            snr_ref[pl.ds(8 * devices * m + c, 8, stride=devices), :] = ratio

    def finish_both(i, _):
        finish(2 * i)
        finish(2 * i + 1)
        return 0

    lax.fori_loop(0, rows // 16, finish_both, 0)

    peak = snr_ref[...].T[:8]
    trial = me * chan + lax.broadcasted_iota(jnp.int32, (8, chan), 1)
    peak = jnp.where(trial < lim_ref[0], peak, 0.0)
    beam_ref[my_beam] = peak
    copies = []
    for o in range(1, beams):
        copy = pltpu.make_async_remote_copy(
            src_ref=beam_ref.at[my_beam],
            dst_ref=beam_ref.at[my_beam],
            send_sem=bsend_sem.at[o],
            recv_sem=brecv_sem.at[o],
            device_id={"beam": lax.rem(my_beam + o, beams)},
            device_id_type=MESH_ID,
        )
        copy.start()
        copies.append(copy)
    peak_ref[0] = peak[:WIDTHS]
    for copy in copies:
        copy.wait()
    total = beam_ref[0]
    for b in range(1, beams):
        total = total + beam_ref[b]
    excess_ref[0] = (peak - total / beams)[:WIDTHS]


def fused_local(devices, beams, block_samples, tail_samples, tail_blocks, dm_limit):
    _, chan, block_len = block_samples.shape
    tail_len = tail_samples.shape[2]
    levels = chan.bit_length() - 1
    cross = devices.bit_length() - 1
    tail_tiles, block_tiles = tail_len // LANES, block_len // LANES
    win = windows(levels + cross, block_len + 2 ** (WIDTHS - 1) - 1, tail_tiles + block_tiles)
    rows = chan // devices
    scratch = [pltpu.VMEM((win[0], chan, LANES), jnp.float32)]
    for s in range(1, levels - 3):
        scratch.append(
            pltpu.VMEM((1 << (levels - 3 - s), 1 << s, win[s], 8, LANES), jnp.float32)
        )
    tiles = win[levels]
    scratch += [
        pltpu.VMEM((tiles, chan, LANES), jnp.float32),
        pltpu.VMEM((devices, tiles, rows, LANES), jnp.float32),
        pltpu.VMEM((devices, tiles, rows, LANES), jnp.float32),
        pltpu.VMEM((chan, LANES), jnp.float32),
        pltpu.VMEM((beams, 8, chan), jnp.float32),
        pltpu.VMEM((chan, tail_len + block_len), jnp.bfloat16),
        pltpu.SemaphoreType.DMA((tail_len // PIECE + 1,)),
        pltpu.SemaphoreType.DMA((devices,)),
        pltpu.SemaphoreType.DMA((devices,)),
        pltpu.SemaphoreType.DMA((beams,)),
        pltpu.SemaphoreType.DMA((beams,)),
    ]
    out = jax.ShapeDtypeStruct((1, WIDTHS, chan), jnp.float32)
    return pl.pallas_call(
        functools.partial(fused, levels, cross, devices, beams, win, tail_tiles, block_tiles),
        out_shape=(out, out),
        in_specs=[pl.BlockSpec(memory_space=pltpu.SMEM)] * 2
        + [pl.BlockSpec(memory_space=pltpu.HBM)] * 2,
        out_specs=(pl.BlockSpec(memory_space=pltpu.VMEM),) * 2,
        scratch_shapes=scratch,
        compiler_params=pltpu.CompilerParams(
            collective_id=0, has_side_effects=True, vmem_limit_bytes=48 * 2**20
        ),
    )(tail_blocks, dm_limit, block_samples, tail_samples)


def fits(devices, beams_all, beams, chan):
    return beams_all == beams and chan % (16 * devices) == 0 and chan <= 64 * devices and chan >= 64


def solution(mesh):
    devices, beams = mesh.shape["freq"], mesh.shape["beam"]

    def body(block_samples, tail_samples, tail_blocks, dm_limit):
        args = (block_samples, tail_samples, tail_blocks, dm_limit)
        if fits(devices, beams * block_samples.shape[0], beams, block_samples.shape[1]):
            return fused_local(devices, beams, *args)
        return local(*args)

    return jax.shard_map(
        body,
        mesh=mesh,
        in_specs=(P("beam", "freq", None), P("beam", "freq", None), P("beam"), P("beam")),
        out_specs=(P("beam", None, "freq"), P("beam", None, "freq")),
        check_vma=False,
    )
```

```python
import functools

import jax
import jax.numpy as jnp
import numpy as np
from jax import lax
from jax.experimental import pallas as pl
from jax.experimental.pallas import tpu as pltpu
from jax.sharding import PartitionSpec as P

WIDTHS = 7


def partner_2(block, axis, stride):
    count = lax.axis_size(axis)
    route = []
    for low in range(count):
        high = low | 1 << stride
        if high != low and high < count:
            route += [(low, high), (high, low)]
    return lax.ppermute(block, axis, route)


def skew_rows(series, step_size, base_shift, pad_width):
    dims_of = series.shape
    rows_count = dims_of[-2]
    length_now = dims_of[-1]
    flattened = series.reshape((-1, rows_count, length_now))
    padded = jnp.pad(flattened, ((0, 0), (0, 0), (pad_width, 0)))
    row_width = length_now + pad_width
    lined_up = padded.reshape((flattened.shape[0], rows_count * row_width))
    lined_up = jnp.pad(lined_up, ((0, 0), (0, pad_width)))
    window = lax.dynamic_slice_in_dim(
        lined_up, pad_width - base_shift, rows_count * (row_width - step_size), axis=1
    )
    moved_rows = window.reshape((flattened.shape[0], rows_count, row_width - step_size))[
        :, :, :length_now
    ]
    return moved_rows.reshape(dims_of)


def tree_section(series, offset, reach_max):
    upper_rows = series[..., 0::2, :, :]
    odd_rows = series[..., 1::2, :, :]
    even_moved = skew_rows(odd_rows, 1, (offset + 1) // 2, reach_max)
    odd_moved = skew_rows(odd_rows, 1, (offset + 2) // 2, reach_max)
    joined_rows = jnp.stack([upper_rows + even_moved, upper_rows + odd_moved], axis=-2)
    dims_of = upper_rows.shape
    return joined_rows.reshape(dims_of[:-2] + (2 * dims_of[-2], dims_of[-1]))


def peak_ratios(series, tail_len):
    searched = series[..., tail_len:]
    average = jnp.mean(searched, axis=-1, keepdims=True)
    deviation = jnp.sqrt(jnp.mean((searched - average) ** 2, axis=-1, keepdims=True) + 1e-05)
    reach_back = 2 ** (WIDTHS - 1)
    boxcar = series[..., tail_len - reach_back :]
    results = []
    for width_bit in range(WIDTHS):
        width_now = 2**width_bit
        if width_bit > 0:
            half_width = width_now // 2
            pad_spec = [(0, 0)] * (series.ndim - 1) + [(half_width, 0)]
            boxcar = boxcar + jnp.pad(boxcar[..., :-half_width], pad_spec)
        ratio = (boxcar[..., reach_back:] - width_now * average) / (
            jnp.sqrt(jnp.float32(width_now)) * deviation
        )
        results.append(jnp.max(ratio, axis=-1))
    return jnp.stack(results, axis=-2)


def local(block_samples, tail_samples, tail_blocks, dm_limit):
    beams_dev, local_chan, block_len = block_samples.shape
    tail_len = tail_samples.shape[2]
    valid_mask = (
        jnp.arange(tail_len, dtype=jnp.int32)[None, None, :]
        >= tail_len - 128 * tail_blocks[:, None, None]
    )
    joined = jnp.concatenate(
        [
            jnp.where(valid_mask, tail_samples.astype(jnp.float32), jnp.float32(0.0)),
            block_samples.astype(jnp.float32),
        ],
        axis=-1,
    )
    series = joined[:, :, None, :]
    while series.shape[1] > 1:
        series = tree_section(series, 0, series.shape[2])
    devices = lax.axis_size("freq")
    position = lax.axis_index("freq")
    level_count = devices.bit_length() - 1
    dm_rows = series[:, 0]
    rank_now = jnp.zeros((), jnp.int32)
    for level_bit in range(level_count):
        group_size = 1 << level_bit
        partner = partner_2(dm_rows, "freq", level_bit)
        side_bit = position // group_size % 2
        rank_now = 2 * rank_now + side_bit
        mine_first = side_bit == 0
        upper_half = jnp.where(mine_first, dm_rows, partner)
        lower_half = jnp.where(mine_first, partner, dm_rows)
        base_shift = (rank_now + 1) // 2
        dm_rows = upper_half + skew_rows(
            lower_half, group_size, base_shift, group_size * local_chan
        )
    scores = peak_ratios(dm_rows, tail_len)
    received = lax.all_to_all(scores[..., None], "freq", split_axis=2, concat_axis=3, tiled=True)
    sources = np.arange(devices)
    reorder = np.zeros(devices, dtype=np.int32)
    for level_bit in range(level_count):
        reorder = reorder + ((sources >> level_bit & 1) << level_count - 1 - level_bit).astype(
            np.int32
        )
    received = jnp.take(received, jnp.asarray(reorder), axis=3)
    scores = received.reshape((beams_dev, WIDTHS, local_chan))
    trial_ids = position * local_chan + jnp.arange(local_chan, dtype=jnp.int32)
    peak_snr = jnp.where(
        trial_ids[None, None, :] < dm_limit[:, None, None], scores, jnp.float32(0.0)
    )
    beam_total = lax.psum(jnp.sum(peak_snr, axis=0), "beam")
    excess_snr = peak_snr - beam_total[None] / (beams_dev * lax.axis_size("beam"))
    return (peak_snr, excess_snr)


LANES = 128
PIECE = 256
SPLITS = 3
AT_ONCE = (2, 4, 4, 4, 4)
MESH_ID = pl.DeviceIdType.MESH


def windows(levels, devices, keep):
    need = [0] * (levels + 1)
    need[levels] = keep + devices - 1
    for s in reversed(range(levels)):
        unit = 1 << (levels - 1 - s)
        if s >= levels - 3:
            need[s] = need[s + 1] + devices * unit
        else:
            start = need[s + 1]
            if s == levels - 4:
                start += 7 * ((1 << (levels - 3)) - 1)
                need[s + 1] = start
            need[s] = start + (devices - 1) * unit + unit // 8
    return [-(-n // LANES) for n in need]


def late_tiles(later, earlier, amount):
    lane = lax.broadcasted_iota(jnp.int32, (8, LANES), 1)
    return jnp.where(lane < amount, earlier, later)


def shift_uniform(tiles, amount):
    rolled = [pltpu.roll(x, amount, 1) for x in tiles]
    lane = lax.broadcasted_iota(jnp.int32, (8, LANES), 1)
    head = lane < amount
    return [
        jnp.where(head, rolled[max(i - 1, 0)], rolled[i]) for i in range(len(tiles))
    ]


def merge_uniform(first, second, amount):
    even = [a + b for a, b in zip(first, second)]
    if isinstance(amount, int) and amount == 0:
        late_first = first
    else:
        late_first = shift_uniform(first, amount)
    late_second = shift_uniform(second, amount + 1)
    odd = [a + b for a, b in zip(late_first, late_second)]
    return even, odd


def fused(
    levels,
    cross,
    devices,
    beams,
    win,
    tail_tiles,
    block_tiles,
    tb_ref,
    lim_ref,
    block_ref,
    tail_ref,
    peak_ref,
    excess_ref,
    split_ref,
    *rest,
):
    stage_refs = rest[: levels - 4]
    turn_ref, send_ref, recv_ref, snr_ref, beam_ref, held_ref = rest[levels - 4 : levels + 2]
    load_sem, send_sem, recv_sem, bsend_sem, brecv_sem = rest[levels + 2 :]
    me = lax.axis_index("freq")
    my_beam = lax.axis_index("beam")
    chan = 1 << levels
    half = chan // 2
    rows = chan // devices
    tail_len, block_len = tail_tiles * LANES, block_tiles * LANES
    pieces = [(tail_ref, at, at, PIECE) for at in range(0, tail_len, PIECE)]
    pieces += [(block_ref, at, tail_len + at, PIECE) for at in range(0, block_len, PIECE)]
    loads = []
    for i, (source, at, to, size) in enumerate(pieces):
        load = pltpu.make_async_copy(
            source.at[0, :, at : at + size], held_ref.at[:, to : to + size], load_sem.at[i]
        )
        load.start()
        loads.append(load)

    barrier = pltpu.get_barrier_semaphore()
    for o in range(1, devices):
        pl.semaphore_signal(
            barrier, inc=1, device_id={"freq": lax.rem(me + o, devices)}, device_id_type=MESH_ID
        )
    for o in range(1, beams):
        pl.semaphore_signal(
            barrier, inc=1, device_id={"beam": lax.rem(my_beam + o, beams)}, device_id_type=MESH_ID
        )

    groups = half // 8
    row = lax.broadcasted_iota(jnp.int32, (chan, chan), 0)
    col = lax.broadcasted_iota(jnp.int32, (chan, chan), 1)
    inner = row % half
    wanted = 2 * ((inner % 8) * groups + inner // 8) + row // half
    pick = jnp.where(col == wanted, 1.0, 0.0).astype(jnp.bfloat16)
    first_valid = tail_tiles - tb_ref[0]
    fill = split_ref.shape[0] - tail_tiles - block_tiles
    split_ref[:fill] = jnp.zeros((fill, chan, LANES), jnp.float32)

    def split(i, _):
        for k in range(SPLITS):
            at = pl.multiple_of((SPLITS * i + k) * PIECE, PIECE)
            piece = held_ref.at[:, pl.ds(at, PIECE)]
            pltpu.make_async_copy(
                block_ref.at[0, :, :PIECE], piece, load_sem.at[SPLITS * i + k]
            ).wait()
            part = jnp.dot(pick, piece[...], preferred_element_type=jnp.float32)
            for h in range(PIECE // LANES):
                tile = (SPLITS * i + k) * (PIECE // LANES) + h
                gain = jnp.where(tile >= first_valid, 1.0, 0.0).astype(jnp.float32)
                split_ref[fill + tile] = part[:, LANES * h : LANES * (h + 1)] * gain
        return 0

    lax.fori_loop(0, len(pieces) // SPLITS, split, 0)

    for ref in stage_refs:
        ref[:, :, 0] = jnp.zeros((ref.shape[0], ref.shape[1], 8, LANES), jnp.float32)
    lane_row = lax.broadcasted_iota(jnp.int32, (8, LANES), 1)
    for s in range(levels - 3):
        out_groups = 1 << (levels - 4 - s)
        out_tiles = win[s + 1]
        unit = 1 << (levels - 1 - s)
        trials = 1 << s

        def level_pair(index, s=s, out_tiles=out_tiles, unit=unit, trials=trials):
            g, e = index // trials, index % trials
            if s == 0:
                held_tiles = split_ref.shape[0]

                def load(which, start, count):
                    at = pl.multiple_of(half * which + 8 * g, 8)
                    return split_ref[pl.ds(start, count), pl.ds(at, 8), :]
            else:
                source = stage_refs[s - 1]
                held_tiles = source.shape[2]

                def load(which, start, count):
                    return source[2 * g + which, e, pl.ds(start, count)]

            low = held_tiles - out_tiles
            even = load(0, low, out_tiles) + load(1, low, out_tiles)
            base = me * unit + g
            start, short = low - base // LANES - 1, base % LANES
            first = pltpu.roll(load(0, start, out_tiles + 1), short, 2)
            second = pltpu.roll(load(1, start, out_tiles + 1), short + 1, 2)
            odd = late_tiles(first[1:], first[:-1], short) + late_tiles(
                second[1:], second[:-1], short + 1
            )
            if s + 1 < levels - 3:
                target = stage_refs[s]
                target[g, 2 * e, 1:] = even
                target[g, 2 * e + 1, 1:] = odd
            else:
                at = pl.multiple_of(16 * e, 16)
                turn_ref[:, pl.ds(at, 8)] = even
                turn_ref[:, pl.ds(at + 8, 8)] = odd

        at_once = AT_ONCE[min(s, len(AT_ONCE) - 1)]

        def level_pairs(i, _, level_pair=level_pair, at_once=at_once):
            for k in range(at_once):
                level_pair(at_once * i + k)
            return 0

        lax.fori_loop(0, groups // at_once, level_pairs, 0)

    pl.semaphore_wait(barrier, devices + beams - 2)
    tiles = win[levels]
    per = rows // 8
    dests = 8 // per

    early = win[levels - 3] - tiles
    sublane = lax.broadcasted_iota(jnp.int32, (8, LANES), 0)

    def last_levels(q):
        nodes = []
        for r in range(8):
            base = 8 * r * q
            whole, short = base // LANES, base % LANES

            def tile(w):
                at = jnp.maximum(w + early - whole, 0)
                x = turn_ref[at, pl.ds(pl.multiple_of(64 * q, 64) + r, 8, stride=8), :]
                return x if r == 0 else pltpu.roll(x, short, 1)

            if r == 0:
                nodes.append([[tile(w) for w in range(tiles)]])
                continue
            moved = [tile(w) for w in range(-2, tiles)]
            moved = [late_tiles(y, x, short) for x, y in zip(moved, moved[1:])]
            moved = [pltpu.roll(x, 0, 1, stride=r, stride_axis=0) for x in moved]
            nodes.append(
                [[late_tiles(y, x, r * sublane) for x, y in zip(moved, moved[1:])]]
            )
        for s in range(3):
            merged = []
            for j in range(len(nodes) // 2):
                amount = me * (4 >> s) + j
                grown = []
                for a, b in zip(nodes[2 * j], nodes[2 * j + 1]):
                    even, odd = merge_uniform(a, b, amount)
                    grown += [even, odd]
                merged.append(grown)
            nodes = merged
        for c in range(8):
            for w in range(tiles):
                for h in range(dests):
                    send_ref[dests * q + h, w, pl.ds(c, per, stride=8), :] = nodes[0][c][w][
                        per * h : per * (h + 1)
                    ]

    def exchange(target, source):
        return pltpu.make_async_remote_copy(
            src_ref=send_ref.at[target],
            dst_ref=recv_ref.at[source],
            send_sem=send_sem.at[target],
            recv_sem=recv_sem.at[source],
            device_id={"freq": target},
            device_id_type=MESH_ID,
        )

    chunks = chan // 64

    def chunk(i, _):
        q = lax.rem(me // dests + i, chunks)
        last_levels(q)
        for h in range(dests):
            target = dests * q + h

            @pl.when(target != me)
            def _():
                exchange(target, me).start()

        return 0

    lax.fori_loop(1, chunks + 1, chunk, 0)
    recv_ref[me] = send_ref[me]
    for o in range(1, devices):
        other = lax.rem(me + o, devices)
        exchange(other, me).wait_send()
        exchange(other, other).wait_recv()

    lane = lax.broadcasted_iota(jnp.int32, (8, LANES), 1)
    widths = jnp.ones((8, LANES), jnp.float32)
    roots = jnp.ones((8, LANES), jnp.float32)
    for i in range(WIDTHS):
        widths = jnp.where(lane == i, jnp.float32(2**i), widths)
        roots = jnp.where(lane == i, jnp.sqrt(jnp.float32(2**i)), roots)
    samples = block_tiles * LANES

    def finish(m, _):
        nodes = [
            [
                [recv_ref[j, w, pl.ds(pl.multiple_of(8 * m, 8), 8), :] for w in range(tiles)]
            ]
            for j in range(devices)
        ]
        for s in range(cross):
            merged = []
            for j in range(len(nodes) // 2):
                grown = []
                for a, b in zip(nodes[2 * j], nodes[2 * j + 1]):
                    even, odd = merge_uniform(a, b, j)
                    grown += [even, odd]
                merged.append(grown)
            nodes = merged
        for c in range(devices):
            series = nodes[0][c]
            block = series[tiles - block_tiles :]
            average = jnp.sum(sum(block), axis=1, keepdims=True) / samples
            variance = (
                jnp.sum(sum((x - average) ** 2 for x in block), axis=1, keepdims=True) / samples
            )
            deviation = jnp.sqrt(variance + 1e-05)
            peaks = jnp.zeros((8, LANES), jnp.float32)
            box = series
            for i in range(WIDTHS):
                if i > 0:
                    box = [x + y for x, y in zip(box, shift_uniform(box, 2 ** (i - 1)))]
                top = functools.reduce(jnp.maximum, box[tiles - block_tiles :])
                peaks = jnp.where(lane == i, jnp.max(top, axis=1, keepdims=True), peaks)
            ratio = (peaks - widths * average) / (roots * deviation)
            snr_ref[pl.ds(8 * devices * m + c, 8, stride=devices), :] = ratio
        return 0

    lax.fori_loop(0, rows // 8, finish, 0)

    peak = snr_ref[...].T[:8]
    trial = me * chan + lax.broadcasted_iota(jnp.int32, (8, chan), 1)
    peak = jnp.where(trial < lim_ref[0], peak, 0.0)
    beam_ref[my_beam] = peak
    copies = []
    for o in range(1, beams):
        copy = pltpu.make_async_remote_copy(
            src_ref=beam_ref.at[my_beam],
            dst_ref=beam_ref.at[my_beam],
            send_sem=bsend_sem.at[o],
            recv_sem=brecv_sem.at[o],
            device_id={"beam": lax.rem(my_beam + o, beams)},
            device_id_type=MESH_ID,
        )
        copy.start()
        copies.append(copy)
    peak_ref[0] = peak[:WIDTHS]
    for copy in copies:
        copy.wait()
    total = beam_ref[0]
    for b in range(1, beams):
        total = total + beam_ref[b]
    excess_ref[0] = (peak - total / beams)[:WIDTHS]


def fused_local(devices, beams, block_samples, tail_samples, tail_blocks, dm_limit):
    _, chan, block_len = block_samples.shape
    tail_len = tail_samples.shape[2]
    levels = chan.bit_length() - 1
    cross = devices.bit_length() - 1
    tail_tiles, block_tiles = tail_len // LANES, block_len // LANES
    win = windows(levels, devices, block_len + 2 ** (WIDTHS - 1) - 1)
    rows = chan // devices
    scratch = [pltpu.VMEM((win[0] + 1, chan, LANES), jnp.float32)]
    for s in range(1, levels - 3):
        scratch.append(
            pltpu.VMEM((1 << (levels - 3 - s), 1 << s, win[s] + 1, 8, LANES), jnp.float32)
        )
    tiles = win[levels]
    scratch += [
        pltpu.VMEM((win[levels - 3], chan, LANES), jnp.float32),
        pltpu.VMEM((devices, tiles, rows, LANES), jnp.float32),
        pltpu.VMEM((devices, tiles, rows, LANES), jnp.float32),
        pltpu.VMEM((chan, LANES), jnp.float32),
        pltpu.VMEM((beams, 8, chan), jnp.float32),
        pltpu.VMEM((chan, tail_len + block_len), jnp.bfloat16),
        pltpu.SemaphoreType.DMA(((tail_len + block_len) // PIECE,)),
        pltpu.SemaphoreType.DMA((devices,)),
        pltpu.SemaphoreType.DMA((devices,)),
        pltpu.SemaphoreType.DMA((beams,)),
        pltpu.SemaphoreType.DMA((beams,)),
    ]
    out = jax.ShapeDtypeStruct((1, WIDTHS, chan), jnp.float32)
    return pl.pallas_call(
        functools.partial(fused, levels, cross, devices, beams, win, tail_tiles, block_tiles),
        out_shape=(out, out),
        in_specs=[pl.BlockSpec(memory_space=pltpu.SMEM)] * 2
        + [pl.BlockSpec(memory_space=pltpu.HBM)] * 2,
        out_specs=(pl.BlockSpec(memory_space=pltpu.VMEM),) * 2,
        scratch_shapes=scratch,
        compiler_params=pltpu.CompilerParams(
            collective_id=0, has_side_effects=True, vmem_limit_bytes=60 * 2**20
        ),
    )(tail_blocks, dm_limit, block_samples, tail_samples)


def fits(devices, beams_all, beams, chan):
    return beams_all == beams and chan % (16 * devices) == 0 and chan <= 64 * devices and chan >= 64


def solution(mesh):
    devices, beams = mesh.shape["freq"], mesh.shape["beam"]

    def body(block_samples, tail_samples, tail_blocks, dm_limit):
        args = (block_samples, tail_samples, tail_blocks, dm_limit)
        if fits(devices, beams * block_samples.shape[0], beams, block_samples.shape[1]):
            return fused_local(devices, beams, *args)
        return local(*args)

    return jax.shard_map(
        body,
        mesh=mesh,
        in_specs=(P("beam", "freq", None), P("beam", "freq", None), P("beam"), P("beam")),
        out_specs=(P("beam", None, "freq"), P("beam", None, "freq")),
        check_vma=False,
    )
```

```python
import functools

import jax
import jax.numpy as jnp
import numpy as np
from jax import lax
from jax.experimental import pallas as pl
from jax.experimental.pallas import tpu as pltpu
from jax.sharding import PartitionSpec as P

WIDTHS = 7


def partner_2(block, axis, stride):
    count = lax.axis_size(axis)
    route = []
    for low in range(count):
        high = low | 1 << stride
        if high != low and high < count:
            route += [(low, high), (high, low)]
    return lax.ppermute(block, axis, route)


def skew_rows(series, step_size, base_shift, pad_width):
    dims_of = series.shape
    rows_count = dims_of[-2]
    length_now = dims_of[-1]
    flattened = series.reshape((-1, rows_count, length_now))
    padded = jnp.pad(flattened, ((0, 0), (0, 0), (pad_width, 0)))
    row_width = length_now + pad_width
    lined_up = padded.reshape((flattened.shape[0], rows_count * row_width))
    lined_up = jnp.pad(lined_up, ((0, 0), (0, pad_width)))
    window = lax.dynamic_slice_in_dim(
        lined_up, pad_width - base_shift, rows_count * (row_width - step_size), axis=1
    )
    moved_rows = window.reshape((flattened.shape[0], rows_count, row_width - step_size))[
        :, :, :length_now
    ]
    return moved_rows.reshape(dims_of)


def tree_section(series, offset, reach_max):
    upper_rows = series[..., 0::2, :, :]
    odd_rows = series[..., 1::2, :, :]
    even_moved = skew_rows(odd_rows, 1, (offset + 1) // 2, reach_max)
    odd_moved = skew_rows(odd_rows, 1, (offset + 2) // 2, reach_max)
    joined_rows = jnp.stack([upper_rows + even_moved, upper_rows + odd_moved], axis=-2)
    dims_of = upper_rows.shape
    return joined_rows.reshape(dims_of[:-2] + (2 * dims_of[-2], dims_of[-1]))


def peak_ratios(series, tail_len):
    searched = series[..., tail_len:]
    average = jnp.mean(searched, axis=-1, keepdims=True)
    deviation = jnp.sqrt(jnp.mean((searched - average) ** 2, axis=-1, keepdims=True) + 1e-05)
    reach_back = 2 ** (WIDTHS - 1)
    boxcar = series[..., tail_len - reach_back :]
    results = []
    for width_bit in range(WIDTHS):
        width_now = 2**width_bit
        if width_bit > 0:
            half_width = width_now // 2
            pad_spec = [(0, 0)] * (series.ndim - 1) + [(half_width, 0)]
            boxcar = boxcar + jnp.pad(boxcar[..., :-half_width], pad_spec)
        ratio = (boxcar[..., reach_back:] - width_now * average) / (
            jnp.sqrt(jnp.float32(width_now)) * deviation
        )
        results.append(jnp.max(ratio, axis=-1))
    return jnp.stack(results, axis=-2)


def local(block_samples, tail_samples, tail_blocks, dm_limit):
    beams_dev, local_chan, block_len = block_samples.shape
    tail_len = tail_samples.shape[2]
    valid_mask = (
        jnp.arange(tail_len, dtype=jnp.int32)[None, None, :]
        >= tail_len - 128 * tail_blocks[:, None, None]
    )
    joined = jnp.concatenate(
        [
            jnp.where(valid_mask, tail_samples.astype(jnp.float32), jnp.float32(0.0)),
            block_samples.astype(jnp.float32),
        ],
        axis=-1,
    )
    series = joined[:, :, None, :]
    while series.shape[1] > 1:
        series = tree_section(series, 0, series.shape[2])
    devices = lax.axis_size("freq")
    position = lax.axis_index("freq")
    level_count = devices.bit_length() - 1
    dm_rows = series[:, 0]
    rank_now = jnp.zeros((), jnp.int32)
    for level_bit in range(level_count):
        group_size = 1 << level_bit
        partner = partner_2(dm_rows, "freq", level_bit)
        side_bit = position // group_size % 2
        rank_now = 2 * rank_now + side_bit
        mine_first = side_bit == 0
        upper_half = jnp.where(mine_first, dm_rows, partner)
        lower_half = jnp.where(mine_first, partner, dm_rows)
        base_shift = (rank_now + 1) // 2
        dm_rows = upper_half + skew_rows(
            lower_half, group_size, base_shift, group_size * local_chan
        )
    scores = peak_ratios(dm_rows, tail_len)
    received = lax.all_to_all(scores[..., None], "freq", split_axis=2, concat_axis=3, tiled=True)
    sources = np.arange(devices)
    reorder = np.zeros(devices, dtype=np.int32)
    for level_bit in range(level_count):
        reorder = reorder + ((sources >> level_bit & 1) << level_count - 1 - level_bit).astype(
            np.int32
        )
    received = jnp.take(received, jnp.asarray(reorder), axis=3)
    scores = received.reshape((beams_dev, WIDTHS, local_chan))
    trial_ids = position * local_chan + jnp.arange(local_chan, dtype=jnp.int32)
    peak_snr = jnp.where(
        trial_ids[None, None, :] < dm_limit[:, None, None], scores, jnp.float32(0.0)
    )
    beam_total = lax.psum(jnp.sum(peak_snr, axis=0), "beam")
    excess_snr = peak_snr - beam_total[None] / (beams_dev * lax.axis_size("beam"))
    return (peak_snr, excess_snr)


LANES = 128
PIECE = 256
SPLITS = 3
AT_ONCE = (2, 2, 4, 4, 4)
MESH_ID = pl.DeviceIdType.MESH


def windows(levels, devices, keep):
    need = [0] * (levels + 1)
    need[levels] = keep + devices - 1
    for s in reversed(range(levels)):
        unit = 1 << (levels - 1 - s)
        if s >= levels - 3:
            need[s] = need[s + 1] + devices * unit
        else:
            start = need[s + 1]
            if s == levels - 4:
                start += 7 * ((1 << (levels - 3)) - 1)
                need[s + 1] = start
            need[s] = start + (devices - 1) * unit + unit // 8
    return [-(-n // LANES) for n in need]


def late_tiles(later, earlier, amount):
    lane = lax.broadcasted_iota(jnp.int32, (8, LANES), 1)
    return jnp.where(lane < amount, earlier, later)


def shift_uniform(tiles, amount):
    rolled = [pltpu.roll(x, amount, 1) for x in tiles]
    lane = lax.broadcasted_iota(jnp.int32, (8, LANES), 1)
    head = lane < amount
    return [
        jnp.where(head, rolled[max(i - 1, 0)], rolled[i]) for i in range(len(tiles))
    ]


def merge_uniform(first, second, amount):
    even = [a + b for a, b in zip(first, second)]
    if isinstance(amount, int) and amount == 0:
        late_first = first
    else:
        late_first = shift_uniform(first, amount)
    late_second = shift_uniform(second, amount + 1)
    odd = [a + b for a, b in zip(late_first, late_second)]
    return even, odd


def fused(
    levels,
    cross,
    devices,
    beams,
    win,
    tail_tiles,
    block_tiles,
    tb_ref,
    lim_ref,
    block_ref,
    tail_ref,
    peak_ref,
    excess_ref,
    split_ref,
    *rest,
):
    stage_refs = rest[: levels - 4]
    turn_ref, send_ref, recv_ref, snr_ref, beam_ref, held_ref = rest[levels - 4 : levels + 2]
    load_sem, send_sem, recv_sem, bsend_sem, brecv_sem = rest[levels + 2 :]
    me = lax.axis_index("freq")
    my_beam = lax.axis_index("beam")
    chan = 1 << levels
    half = chan // 2
    rows = chan // devices
    tail_len, block_len = tail_tiles * LANES, block_tiles * LANES
    pieces = [(tail_ref, at, at, PIECE) for at in range(0, tail_len, PIECE)]
    pieces += [(block_ref, at, tail_len + at, PIECE) for at in range(0, block_len, PIECE)]
    loads = []
    for i, (source, at, to, size) in enumerate(pieces):
        load = pltpu.make_async_copy(
            source.at[0, :, at : at + size], held_ref.at[:, to : to + size], load_sem.at[i]
        )
        load.start()
        loads.append(load)

    barrier = pltpu.get_barrier_semaphore()
    for o in range(1, devices):
        pl.semaphore_signal(
            barrier, inc=1, device_id={"freq": lax.rem(me + o, devices)}, device_id_type=MESH_ID
        )
    for o in range(1, beams):
        pl.semaphore_signal(
            barrier, inc=1, device_id={"beam": lax.rem(my_beam + o, beams)}, device_id_type=MESH_ID
        )

    groups = half // 8
    row = lax.broadcasted_iota(jnp.int32, (chan, chan), 0)
    col = lax.broadcasted_iota(jnp.int32, (chan, chan), 1)
    inner = row % half
    wanted = 2 * ((inner % 8) * groups + inner // 8) + row // half
    pick = jnp.where(col == wanted, 1.0, 0.0).astype(jnp.bfloat16)
    first_valid = tail_tiles - tb_ref[0]
    fill = split_ref.shape[0] - tail_tiles - block_tiles
    split_ref[:fill] = jnp.zeros((fill, chan, LANES), jnp.float32)

    def split(i, _):
        for k in range(SPLITS):
            at = pl.multiple_of((SPLITS * i + k) * PIECE, PIECE)
            pltpu.make_async_copy(
                block_ref.at[0, :, :PIECE],
                held_ref.at[:, pl.ds(at, PIECE)],
                load_sem.at[SPLITS * i + k],
            ).wait()
        wide = SPLITS * PIECE
        part = jnp.dot(
            pick,
            held_ref[:, pl.ds(pl.multiple_of(wide * i, wide), wide)],
            preferred_element_type=jnp.float32,
        )
        for h in range(wide // LANES):
            tile = i * (wide // LANES) + h
            gain = jnp.where(tile >= first_valid, 1.0, 0.0).astype(jnp.float32)
            split_ref[fill + tile] = part[:, LANES * h : LANES * (h + 1)] * gain
        return 0

    lax.fori_loop(0, len(pieces) // SPLITS, split, 0)

    for ref in stage_refs:
        ref[:, :, 0] = jnp.zeros((ref.shape[0], ref.shape[1], 8, LANES), jnp.float32)
    lane_row = lax.broadcasted_iota(jnp.int32, (8, LANES), 1)
    for s in range(levels - 3):
        out_groups = 1 << (levels - 4 - s)
        out_tiles = win[s + 1]
        unit = 1 << (levels - 1 - s)
        trials = 1 << s

        def level_pair(index, s=s, out_tiles=out_tiles, unit=unit, trials=trials):
            g, e = index // trials, index % trials
            if s == 0:
                held_tiles = split_ref.shape[0]

                def load(which, start, count):
                    at = pl.multiple_of(half * which + 8 * g, 8)
                    return split_ref[pl.ds(start, count), pl.ds(at, 8), :]
            else:
                source = stage_refs[s - 1]
                held_tiles = source.shape[2]

                def load(which, start, count):
                    return source[2 * g + which, e, pl.ds(start, count)]

            low = held_tiles - out_tiles
            even = load(0, low, out_tiles) + load(1, low, out_tiles)
            base = me * unit + g
            start, short = low - base // LANES - 1, base % LANES
            first = pltpu.roll(load(0, start, out_tiles + 1), short, 2)
            second = pltpu.roll(load(1, start, out_tiles + 1), short + 1, 2)
            odd = late_tiles(first[1:], first[:-1], short) + late_tiles(
                second[1:], second[:-1], short + 1
            )
            return g, e, even, odd

        def keep_pair(g, e, even, odd, s=s):
            if s + 1 < levels - 3:
                target = stage_refs[s]
                target[g, 2 * e, 1:] = even
                target[g, 2 * e + 1, 1:] = odd
            else:
                at = pl.multiple_of(16 * e, 16)
                turn_ref[:, pl.ds(at, 8)] = even
                turn_ref[:, pl.ds(at + 8, 8)] = odd

        at_once = AT_ONCE[min(s, len(AT_ONCE) - 1)]

        def level_pairs(i, _, level_pair=level_pair, keep_pair=keep_pair, at_once=at_once):
            pairs = [level_pair(at_once * i + k) for k in range(at_once)]
            for pair in pairs:
                keep_pair(*pair)
            return 0

        lax.fori_loop(0, groups // at_once, level_pairs, 0)

    pl.semaphore_wait(barrier, devices + beams - 2)
    tiles = win[levels]
    per = rows // 8
    dests = 8 // per

    early = win[levels - 3] - tiles
    sublane = lax.broadcasted_iota(jnp.int32, (8, LANES), 0)

    def last_levels(q):
        nodes = []
        for r in range(8):
            base = 8 * r * q
            whole, short = base // LANES, base % LANES

            def tile(w):
                at = jnp.maximum(w + early - whole, 0)
                x = turn_ref[at, pl.ds(pl.multiple_of(64 * q, 64) + r, 8, stride=8), :]
                return x if r == 0 else pltpu.roll(x, short, 1)

            if r == 0:
                nodes.append([[tile(w) for w in range(tiles)]])
                continue
            moved = [tile(w) for w in range(-2, tiles)]
            moved = [late_tiles(y, x, short) for x, y in zip(moved, moved[1:])]
            moved = [pltpu.roll(x, 0, 1, stride=r, stride_axis=0) for x in moved]
            nodes.append(
                [[late_tiles(y, x, r * sublane) for x, y in zip(moved, moved[1:])]]
            )
        for s in range(3):
            merged = []
            for j in range(len(nodes) // 2):
                amount = me * (4 >> s) + j
                grown = []
                for a, b in zip(nodes[2 * j], nodes[2 * j + 1]):
                    even, odd = merge_uniform(a, b, amount)
                    grown += [even, odd]
                merged.append(grown)
            nodes = merged
        for c in range(8):
            for w in range(tiles):
                for h in range(dests):
                    send_ref[dests * q + h, w, pl.ds(c, per, stride=8), :] = nodes[0][c][w][
                        per * h : per * (h + 1)
                    ]

    def exchange(target, source):
        return pltpu.make_async_remote_copy(
            src_ref=send_ref.at[target],
            dst_ref=recv_ref.at[source],
            send_sem=send_sem.at[target],
            recv_sem=recv_sem.at[source],
            device_id={"freq": target},
            device_id_type=MESH_ID,
        )

    chunks = chan // 64

    def chunk(i, _):
        q = lax.rem(me // dests + i, chunks)
        last_levels(q)
        for h in range(dests):
            target = dests * q + h

            @pl.when(target != me)
            def _():
                exchange(target, me).start()

        return 0

    lax.fori_loop(1, chunks + 1, chunk, 0)
    recv_ref[me] = send_ref[me]
    for o in range(1, devices):
        other = lax.rem(me + o, devices)
        exchange(other, me).wait_send()
        exchange(other, other).wait_recv()

    lane = lax.broadcasted_iota(jnp.int32, (8, LANES), 1)
    widths = jnp.ones((8, LANES), jnp.float32)
    roots = jnp.ones((8, LANES), jnp.float32)
    for i in range(WIDTHS):
        widths = jnp.where(lane == i, jnp.float32(2**i), widths)
        roots = jnp.where(lane == i, jnp.sqrt(jnp.float32(2**i)), roots)
    samples = block_tiles * LANES

    def finish(m, _):
        nodes = [
            [
                [recv_ref[j, w, pl.ds(pl.multiple_of(8 * m, 8), 8), :] for w in range(tiles)]
            ]
            for j in range(devices)
        ]
        for s in range(cross):
            merged = []
            for j in range(len(nodes) // 2):
                grown = []
                for a, b in zip(nodes[2 * j], nodes[2 * j + 1]):
                    even, odd = merge_uniform(a, b, j)
                    grown += [even, odd]
                merged.append(grown)
            nodes = merged
        for c in range(devices):
            series = nodes[0][c]
            block = series[tiles - block_tiles :]
            average = jnp.sum(sum(block), axis=1, keepdims=True) / samples
            variance = (
                jnp.sum(sum((x - average) ** 2 for x in block), axis=1, keepdims=True) / samples
            )
            deviation = jnp.sqrt(variance + 1e-05)
            peaks = jnp.zeros((8, LANES), jnp.float32)
            box = series
            for i in range(WIDTHS):
                if i > 0:
                    box = [x + y for x, y in zip(box, shift_uniform(box, 2 ** (i - 1)))]
                top = functools.reduce(jnp.maximum, box[tiles - block_tiles :])
                peaks = jnp.where(lane == i, jnp.max(top, axis=1, keepdims=True), peaks)
            ratio = (peaks - widths * average) / (roots * deviation)
            snr_ref[pl.ds(8 * devices * m + c, 8, stride=devices), :] = ratio
        return 0

    lax.fori_loop(0, rows // 8, finish, 0)

    peak = snr_ref[...].T[:8]
    trial = me * chan + lax.broadcasted_iota(jnp.int32, (8, chan), 1)
    peak = jnp.where(trial < lim_ref[0], peak, 0.0)
    beam_ref[my_beam] = peak
    copies = []
    for o in range(1, beams):
        copy = pltpu.make_async_remote_copy(
            src_ref=beam_ref.at[my_beam],
            dst_ref=beam_ref.at[my_beam],
            send_sem=bsend_sem.at[o],
            recv_sem=brecv_sem.at[o],
            device_id={"beam": lax.rem(my_beam + o, beams)},
            device_id_type=MESH_ID,
        )
        copy.start()
        copies.append(copy)
    peak_ref[0] = peak[:WIDTHS]
    for copy in copies:
        copy.wait()
    total = beam_ref[0]
    for b in range(1, beams):
        total = total + beam_ref[b]
    excess_ref[0] = (peak - total / beams)[:WIDTHS]


def fused_local(devices, beams, block_samples, tail_samples, tail_blocks, dm_limit):
    _, chan, block_len = block_samples.shape
    tail_len = tail_samples.shape[2]
    levels = chan.bit_length() - 1
    cross = devices.bit_length() - 1
    tail_tiles, block_tiles = tail_len // LANES, block_len // LANES
    win = windows(levels, devices, block_len + 2 ** (WIDTHS - 1) - 1)
    rows = chan // devices
    scratch = [pltpu.VMEM((win[0] + 1, chan, LANES), jnp.float32)]
    for s in range(1, levels - 3):
        scratch.append(
            pltpu.VMEM((1 << (levels - 3 - s), 1 << s, win[s] + 1, 8, LANES), jnp.float32)
        )
    tiles = win[levels]
    scratch += [
        pltpu.VMEM((win[levels - 3], chan, LANES), jnp.float32),
        pltpu.VMEM((devices, tiles, rows, LANES), jnp.float32),
        pltpu.VMEM((devices, tiles, rows, LANES), jnp.float32),
        pltpu.VMEM((chan, LANES), jnp.float32),
        pltpu.VMEM((beams, 8, chan), jnp.float32),
        pltpu.VMEM((chan, tail_len + block_len), jnp.bfloat16),
        pltpu.SemaphoreType.DMA(((tail_len + block_len) // PIECE,)),
        pltpu.SemaphoreType.DMA((devices,)),
        pltpu.SemaphoreType.DMA((devices,)),
        pltpu.SemaphoreType.DMA((beams,)),
        pltpu.SemaphoreType.DMA((beams,)),
    ]
    out = jax.ShapeDtypeStruct((1, WIDTHS, chan), jnp.float32)
    return pl.pallas_call(
        functools.partial(fused, levels, cross, devices, beams, win, tail_tiles, block_tiles),
        out_shape=(out, out),
        in_specs=[pl.BlockSpec(memory_space=pltpu.SMEM)] * 2
        + [pl.BlockSpec(memory_space=pltpu.HBM)] * 2,
        out_specs=(pl.BlockSpec(memory_space=pltpu.VMEM),) * 2,
        scratch_shapes=scratch,
        compiler_params=pltpu.CompilerParams(
            collective_id=0, has_side_effects=True, vmem_limit_bytes=60 * 2**20
        ),
    )(tail_blocks, dm_limit, block_samples, tail_samples)


def fits(devices, beams_all, beams, chan):
    return beams_all == beams and chan % (16 * devices) == 0 and chan <= 64 * devices and chan >= 64


def solution(mesh):
    devices, beams = mesh.shape["freq"], mesh.shape["beam"]

    def body(block_samples, tail_samples, tail_blocks, dm_limit):
        args = (block_samples, tail_samples, tail_blocks, dm_limit)
        if fits(devices, beams * block_samples.shape[0], beams, block_samples.shape[1]):
            return fused_local(devices, beams, *args)
        return local(*args)

    return jax.shard_map(
        body,
        mesh=mesh,
        in_specs=(P("beam", "freq", None), P("beam", "freq", None), P("beam"), P("beam")),
        out_specs=(P("beam", None, "freq"), P("beam", None, "freq")),
        check_vma=False,
    )
```

```python
import functools

import jax
import jax.numpy as jnp
import numpy as np
from jax import lax
from jax.experimental import pallas as pl
from jax.experimental.pallas import tpu as pltpu
from jax.sharding import PartitionSpec as P

WIDTHS = 7


def partner_2(block, axis, stride):
    count = lax.axis_size(axis)
    route = []
    for low in range(count):
        high = low | 1 << stride
        if high != low and high < count:
            route += [(low, high), (high, low)]
    return lax.ppermute(block, axis, route)


def skew_rows(series, step_size, base_shift, pad_width):
    dims_of = series.shape
    rows_count = dims_of[-2]
    length_now = dims_of[-1]
    flattened = series.reshape((-1, rows_count, length_now))
    padded = jnp.pad(flattened, ((0, 0), (0, 0), (pad_width, 0)))
    row_width = length_now + pad_width
    lined_up = padded.reshape((flattened.shape[0], rows_count * row_width))
    lined_up = jnp.pad(lined_up, ((0, 0), (0, pad_width)))
    window = lax.dynamic_slice_in_dim(
        lined_up, pad_width - base_shift, rows_count * (row_width - step_size), axis=1
    )
    moved_rows = window.reshape((flattened.shape[0], rows_count, row_width - step_size))[
        :, :, :length_now
    ]
    return moved_rows.reshape(dims_of)


def tree_section(series, offset, reach_max):
    upper_rows = series[..., 0::2, :, :]
    odd_rows = series[..., 1::2, :, :]
    even_moved = skew_rows(odd_rows, 1, (offset + 1) // 2, reach_max)
    odd_moved = skew_rows(odd_rows, 1, (offset + 2) // 2, reach_max)
    joined_rows = jnp.stack([upper_rows + even_moved, upper_rows + odd_moved], axis=-2)
    dims_of = upper_rows.shape
    return joined_rows.reshape(dims_of[:-2] + (2 * dims_of[-2], dims_of[-1]))


def peak_ratios(series, tail_len):
    searched = series[..., tail_len:]
    average = jnp.mean(searched, axis=-1, keepdims=True)
    deviation = jnp.sqrt(jnp.mean((searched - average) ** 2, axis=-1, keepdims=True) + 1e-05)
    reach_back = 2 ** (WIDTHS - 1)
    boxcar = series[..., tail_len - reach_back :]
    results = []
    for width_bit in range(WIDTHS):
        width_now = 2**width_bit
        if width_bit > 0:
            half_width = width_now // 2
            pad_spec = [(0, 0)] * (series.ndim - 1) + [(half_width, 0)]
            boxcar = boxcar + jnp.pad(boxcar[..., :-half_width], pad_spec)
        ratio = (boxcar[..., reach_back:] - width_now * average) / (
            jnp.sqrt(jnp.float32(width_now)) * deviation
        )
        results.append(jnp.max(ratio, axis=-1))
    return jnp.stack(results, axis=-2)


def local(block_samples, tail_samples, tail_blocks, dm_limit):
    beams_dev, local_chan, block_len = block_samples.shape
    tail_len = tail_samples.shape[2]
    valid_mask = (
        jnp.arange(tail_len, dtype=jnp.int32)[None, None, :]
        >= tail_len - 128 * tail_blocks[:, None, None]
    )
    joined = jnp.concatenate(
        [
            jnp.where(valid_mask, tail_samples.astype(jnp.float32), jnp.float32(0.0)),
            block_samples.astype(jnp.float32),
        ],
        axis=-1,
    )
    series = joined[:, :, None, :]
    while series.shape[1] > 1:
        series = tree_section(series, 0, series.shape[2])
    devices = lax.axis_size("freq")
    position = lax.axis_index("freq")
    level_count = devices.bit_length() - 1
    dm_rows = series[:, 0]
    rank_now = jnp.zeros((), jnp.int32)
    for level_bit in range(level_count):
        group_size = 1 << level_bit
        partner = partner_2(dm_rows, "freq", level_bit)
        side_bit = position // group_size % 2
        rank_now = 2 * rank_now + side_bit
        mine_first = side_bit == 0
        upper_half = jnp.where(mine_first, dm_rows, partner)
        lower_half = jnp.where(mine_first, partner, dm_rows)
        base_shift = (rank_now + 1) // 2
        dm_rows = upper_half + skew_rows(
            lower_half, group_size, base_shift, group_size * local_chan
        )
    scores = peak_ratios(dm_rows, tail_len)
    received = lax.all_to_all(scores[..., None], "freq", split_axis=2, concat_axis=3, tiled=True)
    sources = np.arange(devices)
    reorder = np.zeros(devices, dtype=np.int32)
    for level_bit in range(level_count):
        reorder = reorder + ((sources >> level_bit & 1) << level_count - 1 - level_bit).astype(
            np.int32
        )
    received = jnp.take(received, jnp.asarray(reorder), axis=3)
    scores = received.reshape((beams_dev, WIDTHS, local_chan))
    trial_ids = position * local_chan + jnp.arange(local_chan, dtype=jnp.int32)
    peak_snr = jnp.where(
        trial_ids[None, None, :] < dm_limit[:, None, None], scores, jnp.float32(0.0)
    )
    beam_total = lax.psum(jnp.sum(peak_snr, axis=0), "beam")
    excess_snr = peak_snr - beam_total[None] / (beams_dev * lax.axis_size("beam"))
    return (peak_snr, excess_snr)


LANES = 128
PIECE = 256
SPLITS = 3
AT_ONCE = (2, 2, 4, 4, 4)
MESH_ID = pl.DeviceIdType.MESH


def windows(levels, devices, keep):
    need = [0] * (levels + 1)
    need[levels] = keep + devices - 1
    for s in reversed(range(levels)):
        unit = 1 << (levels - 1 - s)
        if s >= levels - 3:
            need[s] = need[s + 1] + devices * unit
        else:
            start = need[s + 1]
            if s == levels - 4:
                start += 7 * ((1 << (levels - 3)) - 1)
                need[s + 1] = start
            need[s] = start + (devices - 1) * unit + unit // 8
    return [-(-n // LANES) for n in need]


def late_tiles(later, earlier, amount):
    lane = lax.broadcasted_iota(jnp.int32, (8, LANES), 1)
    return jnp.where(lane < amount, earlier, later)


def shift_uniform(tiles, amount):
    rolled = [pltpu.roll(x, amount, 1) for x in tiles]
    lane = lax.broadcasted_iota(jnp.int32, (8, LANES), 1)
    head = lane < amount
    return [
        jnp.where(head, rolled[max(i - 1, 0)], rolled[i]) for i in range(len(tiles))
    ]


def merge_uniform(first, second, amount):
    even = [a + b for a, b in zip(first, second)]
    if isinstance(amount, int) and amount == 0:
        late_first = first
    else:
        late_first = shift_uniform(first, amount)
    late_second = shift_uniform(second, amount + 1)
    odd = [a + b for a, b in zip(late_first, late_second)]
    return even, odd


def fused(
    levels,
    cross,
    devices,
    beams,
    win,
    tail_tiles,
    block_tiles,
    tb_ref,
    lim_ref,
    block_ref,
    tail_ref,
    out_ref,
    split_ref,
    *rest,
):
    stage_refs = rest[: levels - 4]
    turn_ref, send_ref, recv_ref, snr_ref, beam_ref, held_ref = rest[levels - 4 : levels + 2]
    load_sem, send_sem, recv_sem, bsend_sem, brecv_sem = rest[levels + 2 :]
    me = lax.axis_index("freq")
    my_beam = lax.axis_index("beam")
    chan = 1 << levels
    half = chan // 2
    rows = chan // devices
    tail_len, block_len = tail_tiles * LANES, block_tiles * LANES
    pieces = [(tail_ref, at, at, PIECE) for at in range(0, tail_len, PIECE)]
    pieces += [(block_ref, at, tail_len + at, PIECE) for at in range(0, block_len, PIECE)]
    loads = []
    for i, (source, at, to, size) in enumerate(pieces):
        load = pltpu.make_async_copy(
            source.at[0, :, at : at + size], held_ref.at[:, to : to + size], load_sem.at[i]
        )
        load.start()
        loads.append(load)

    barrier = pltpu.get_barrier_semaphore()
    for o in range(1, devices):
        pl.semaphore_signal(
            barrier, inc=1, device_id={"freq": lax.rem(me + o, devices)}, device_id_type=MESH_ID
        )
    for o in range(1, beams):
        pl.semaphore_signal(
            barrier, inc=1, device_id={"beam": lax.rem(my_beam + o, beams)}, device_id_type=MESH_ID
        )

    groups = half // 8
    row = lax.broadcasted_iota(jnp.int32, (chan, chan), 0)
    col = lax.broadcasted_iota(jnp.int32, (chan, chan), 1)
    inner = row % half
    wanted = 2 * ((inner % 8) * groups + inner // 8) + row // half
    pick = jnp.where(col == wanted, 1.0, 0.0).astype(jnp.bfloat16)
    first_valid = tail_tiles - tb_ref[0]
    fill = split_ref.shape[0] - tail_tiles - block_tiles
    split_ref[:fill] = jnp.zeros((fill, chan, LANES), jnp.float32)

    def split(i, _):
        for k in range(SPLITS):
            at = pl.multiple_of((SPLITS * i + k) * PIECE, PIECE)
            pltpu.make_async_copy(
                block_ref.at[0, :, :PIECE],
                held_ref.at[:, pl.ds(at, PIECE)],
                load_sem.at[SPLITS * i + k],
            ).wait()
        wide = SPLITS * PIECE
        part = jnp.dot(
            pick,
            held_ref[:, pl.ds(pl.multiple_of(wide * i, wide), wide)],
            preferred_element_type=jnp.float32,
        )
        for h in range(wide // LANES):
            tile = i * (wide // LANES) + h
            gain = jnp.where(tile >= first_valid, 1.0, 0.0).astype(jnp.float32)
            split_ref[fill + tile] = part[:, LANES * h : LANES * (h + 1)] * gain
        return 0

    lax.fori_loop(0, len(pieces) // SPLITS, split, 0)

    for ref in stage_refs:
        ref[:, :, 0] = jnp.zeros((ref.shape[0], ref.shape[1], 8, LANES), jnp.float32)
    lane_row = lax.broadcasted_iota(jnp.int32, (8, LANES), 1)
    later_levels = []
    for s in range(levels - 3):
        out_groups = 1 << (levels - 4 - s)
        out_tiles = win[s + 1]
        unit = 1 << (levels - 1 - s)
        trials = 1 << s

        def level_pair(index, part, s=s, out_tiles=out_tiles, unit=unit, trials=trials):
            count = max(trials // 2, 1)
            g, e = index // count, part * count + index % count
            if s == 0:
                held_tiles = split_ref.shape[0]

                def load(which, start, count):
                    at = pl.multiple_of(half * which + 8 * g, 8)
                    return split_ref[pl.ds(start, count), pl.ds(at, 8), :]
            else:
                source = stage_refs[s - 1]
                held_tiles = source.shape[2]

                def load(which, start, count):
                    return source[2 * g + which, e, pl.ds(start, count)]

            low = held_tiles - out_tiles
            even = load(0, low, out_tiles) + load(1, low, out_tiles)
            base = me * unit + g
            start, short = low - base // LANES - 1, base % LANES
            first = pltpu.roll(load(0, start, out_tiles + 1), short, 2)
            second = pltpu.roll(load(1, start, out_tiles + 1), short + 1, 2)
            odd = late_tiles(first[1:], first[:-1], short) + late_tiles(
                second[1:], second[:-1], short + 1
            )
            return g, e, even, odd

        def keep_pair(g, e, even, odd, s=s):
            if s + 1 < levels - 3:
                target = stage_refs[s]
                target[g, 2 * e, 1:] = even
                target[g, 2 * e + 1, 1:] = odd
            else:
                at = pl.multiple_of(16 * e, 16)
                turn_ref[:, pl.ds(at, 8)] = even
                turn_ref[:, pl.ds(at + 8, 8)] = odd

        at_once = AT_ONCE[min(s, len(AT_ONCE) - 1)]

        def level(part, s=s, level_pair=level_pair, keep_pair=keep_pair, at_once=at_once):
            def level_pairs(i, _):
                pairs = [level_pair(at_once * i + k, part) for k in range(at_once)]
                for pair in pairs:
                    keep_pair(*pair)
                return 0

            lax.fori_loop(0, (groups if s == 0 else groups // 2) // at_once, level_pairs, 0)

        later_levels.append(level)

    tiles = win[levels]
    per = rows // 8
    dests = 8 // per

    early = win[levels - 3] - tiles
    sublane = lax.broadcasted_iota(jnp.int32, (8, LANES), 0)

    def last_levels(q):
        nodes = []
        for r in range(8):
            base = 8 * r * q
            whole, short = base // LANES, base % LANES

            def tile(w):
                at = jnp.maximum(w + early - whole, 0)
                x = turn_ref[at, pl.ds(pl.multiple_of(64 * q, 64) + r, 8, stride=8), :]
                return x if r == 0 else pltpu.roll(x, short, 1)

            if r == 0:
                nodes.append([[tile(w) for w in range(tiles)]])
                continue
            moved = [tile(w) for w in range(-2, tiles)]
            moved = [late_tiles(y, x, short) for x, y in zip(moved, moved[1:])]
            moved = [pltpu.roll(x, 0, 1, stride=r, stride_axis=0) for x in moved]
            nodes.append(
                [[late_tiles(y, x, r * sublane) for x, y in zip(moved, moved[1:])]]
            )
        for s in range(3):
            merged = []
            for j in range(len(nodes) // 2):
                amount = me * (4 >> s) + j
                grown = []
                for a, b in zip(nodes[2 * j], nodes[2 * j + 1]):
                    even, odd = merge_uniform(a, b, amount)
                    grown += [even, odd]
                merged.append(grown)
            nodes = merged
        for c in range(8):
            for w in range(tiles):
                for h in range(dests):
                    send_ref[dests * q + h, w, pl.ds(c, per, stride=8), :] = nodes[0][c][w][
                        per * h : per * (h + 1)
                    ]

    def exchange(target, source):
        return pltpu.make_async_remote_copy(
            src_ref=send_ref.at[target],
            dst_ref=recv_ref.at[source],
            send_sem=send_sem.at[target],
            recv_sem=recv_sem.at[source],
            device_id={"freq": target},
            device_id_type=MESH_ID,
        )

    chunks = chan // 64

    own = me // dests
    chunks_part = chunks // 2

    def half_of_trials(turn, _):
        part = lax.rem(own // chunks_part + 1 + turn, 2)
        for level in later_levels[1:]:
            level(part)

        def chunk(i, _):
            q = part * chunks_part + lax.rem(own % chunks_part + 1 + i, chunks_part)
            last_levels(q)
            for h in range(dests):
                target = dests * q + h

                @pl.when(target != me)
                def _():
                    exchange(target, me).start()

            return 0

        lax.fori_loop(0, chunks_part, chunk, 0)
        return 0

    later_levels[0](0)
    pl.semaphore_wait(barrier, devices + beams - 2)
    lax.fori_loop(0, 2, half_of_trials, 0)
    recv_ref[me] = send_ref[me]
    for o in range(1, devices):
        other = lax.rem(me + o, devices)
        exchange(other, me).wait_send()
        exchange(other, other).wait_recv()

    lane = lax.broadcasted_iota(jnp.int32, (8, LANES), 1)
    widths = jnp.ones((8, LANES), jnp.float32)
    roots = jnp.ones((8, LANES), jnp.float32)
    for i in range(WIDTHS):
        widths = jnp.where(lane == i, jnp.float32(2**i), widths)
        roots = jnp.where(lane == i, jnp.sqrt(jnp.float32(2**i)), roots)
    samples = block_tiles * LANES

    def finish(m, _):
        nodes = [
            [
                [recv_ref[j, w, pl.ds(pl.multiple_of(8 * m, 8), 8), :] for w in range(tiles)]
            ]
            for j in range(devices)
        ]
        for s in range(cross):
            merged = []
            for j in range(len(nodes) // 2):
                grown = []
                for a, b in zip(nodes[2 * j], nodes[2 * j + 1]):
                    even, odd = merge_uniform(a, b, j)
                    grown += [even, odd]
                merged.append(grown)
            nodes = merged
        for c in range(devices):
            series = nodes[0][c]
            block = series[tiles - block_tiles :]
            average = jnp.sum(sum(block), axis=1, keepdims=True) / samples
            variance = (
                jnp.sum(sum((x - average) ** 2 for x in block), axis=1, keepdims=True) / samples
            )
            deviation = jnp.sqrt(variance + 1e-05)
            peaks = jnp.zeros((8, LANES), jnp.float32)
            box = series
            for i in range(WIDTHS):
                if i > 0:
                    box = [x + y for x, y in zip(box, shift_uniform(box, 2 ** (i - 1)))]
                top = functools.reduce(jnp.maximum, box[tiles - block_tiles :])
                peaks = jnp.where(lane == i, jnp.max(top, axis=1, keepdims=True), peaks)
            ratio = (peaks - widths * average) / (roots * deviation)
            snr_ref[pl.ds(8 * devices * m + c, 8, stride=devices), :] = ratio
        return 0

    lax.fori_loop(0, rows // 8, finish, 0)

    peak = snr_ref[...].T[:8]
    trial = me * chan + lax.broadcasted_iota(jnp.int32, (8, chan), 1)
    peak = jnp.where(trial < lim_ref[0], peak, 0.0)
    beam_ref[my_beam] = peak
    copies = []
    for o in range(1, beams):
        copy = pltpu.make_async_remote_copy(
            src_ref=beam_ref.at[my_beam],
            dst_ref=beam_ref.at[my_beam],
            send_sem=bsend_sem.at[o],
            recv_sem=brecv_sem.at[o],
            device_id={"beam": lax.rem(my_beam + o, beams)},
            device_id_type=MESH_ID,
        )
        copy.start()
        copies.append(copy)
    for i in range(8):
        out_ref[i] = peak[i : i + 1]
    for copy in copies:
        copy.wait()
    total = beam_ref[0]
    for b in range(1, beams):
        total = total + beam_ref[b]
    mean = total / beams
    for i in range(8):
        out_ref[8 + i] = mean[i : i + 1]


def fused_local(devices, beams, block_samples, tail_samples, tail_blocks, dm_limit):
    _, chan, block_len = block_samples.shape
    tail_len = tail_samples.shape[2]
    levels = chan.bit_length() - 1
    cross = devices.bit_length() - 1
    tail_tiles, block_tiles = tail_len // LANES, block_len // LANES
    win = windows(levels, devices, block_len + 2 ** (WIDTHS - 1) - 1)
    rows = chan // devices
    scratch = [pltpu.VMEM((win[0] + 1, chan, LANES), jnp.float32)]
    for s in range(1, levels - 3):
        scratch.append(
            pltpu.VMEM((1 << (levels - 3 - s), 1 << s, win[s] + 1, 8, LANES), jnp.float32)
        )
    tiles = win[levels]
    scratch += [
        pltpu.VMEM((win[levels - 3], chan, LANES), jnp.float32),
        pltpu.VMEM((devices, tiles, rows, LANES), jnp.float32),
        pltpu.VMEM((devices, tiles, rows, LANES), jnp.float32),
        pltpu.VMEM((chan, LANES), jnp.float32),
        pltpu.VMEM((beams, 8, chan), jnp.float32),
        pltpu.VMEM((chan, tail_len + block_len), jnp.bfloat16),
        pltpu.SemaphoreType.DMA(((tail_len + block_len) // PIECE,)),
        pltpu.SemaphoreType.DMA((devices,)),
        pltpu.SemaphoreType.DMA((devices,)),
        pltpu.SemaphoreType.DMA((beams,)),
        pltpu.SemaphoreType.DMA((beams,)),
    ]
    both = pl.pallas_call(
        functools.partial(fused, levels, cross, devices, beams, win, tail_tiles, block_tiles),
        out_shape=jax.ShapeDtypeStruct((16, 1, chan), jnp.float32),
        in_specs=[pl.BlockSpec(memory_space=pltpu.SMEM)] * 2
        + [pl.BlockSpec(memory_space=pltpu.HBM)] * 2,
        out_specs=pl.BlockSpec(memory_space=pltpu.VMEM),
        scratch_shapes=scratch,
        compiler_params=pltpu.CompilerParams(
            collective_id=0, has_side_effects=True, vmem_limit_bytes=60 * 2**20
        ),
    )(tail_blocks, dm_limit, block_samples, tail_samples)
    peak, mean = both[:WIDTHS], both[8 : 8 + WIDTHS]
    return jnp.transpose(peak, (1, 0, 2)), jnp.transpose(peak - mean, (1, 0, 2))


def fits(devices, beams_all, beams, chan):
    return beams_all == beams and chan % (16 * devices) == 0 and chan <= 64 * devices and chan >= 128


def solution(mesh):
    devices, beams = mesh.shape["freq"], mesh.shape["beam"]

    def body(block_samples, tail_samples, tail_blocks, dm_limit):
        args = (block_samples, tail_samples, tail_blocks, dm_limit)
        if fits(devices, beams * block_samples.shape[0], beams, block_samples.shape[1]):
            return fused_local(devices, beams, *args)
        return local(*args)

    return jax.shard_map(
        body,
        mesh=mesh,
        in_specs=(P("beam", "freq", None), P("beam", "freq", None), P("beam"), P("beam")),
        out_specs=(P("beam", None, "freq"), P("beam", None, "freq")),
        check_vma=False,
    )
```
